512 devices in a mesh: ctx: 32 (over z, core), exp: 16 (over y, x).
Axes of the slice: x: 4, y: 4, z: 16, core: 2. Of those that a mesh axis runs over, the one named last changes fastest.
Arguments:
- x_in: bfloat16 [4096, 4096], P('ctx', 'exp'), may hold values from -6 to 6
- z_gate: bfloat16 [4096, 4096], P('ctx', 'exp'), may hold values from -6 to 6
- b_proj: bfloat16 [4096, 128], P('ctx'), may hold values from -0.5 to 0.5
- c_proj: bfloat16 [4096, 128], P('ctx'), may hold values from -0.5 to 0.5
- dt_raw: float32 [64, 4096], P('exp', 'ctx'), may hold values from -4 to 4
- a_log: float32 [64], P('exp'), may hold values from -13 to -2.9
- d_skip: float32 [64], P('exp'), may hold values from 0.5 to 1.5
- out_proj: bfloat16 [4096, 2048], P('exp'), may hold values from -0.09375 to 0.09375
- residual: bfloat16 [4096, 2048], P('ctx'), may hold values from -80 to 80
- norm_gain: float32 [2048], replicated, may hold values from 0.5 to 1.5
- router: bfloat16 [2048, 16], replicated, may hold values from -0.125 to 0.125
- w_gate: bfloat16 [16, 2048, 7168], P(None, 'ctx', 'exp'), may hold values from -0.125 to 0.125
- w_up: bfloat16 [16, 2048, 7168], P(None, 'ctx', 'exp'), may hold values from -0.125 to 0.125
- w_down: bfloat16 [16, 2048, 7168], P(None, 'ctx', 'exp'), may hold values from -0.0625 to 0.0625
- block_experts: int32 [32, 2], replicated, may hold values from 0 to 15, all different within a row
Outputs:
- stream_out: bfloat16 [4096, 2048], P('ctx', 'exp')
- expert_out: bfloat16 [4096, 2048], P('ctx', 'exp')
The draws below stay inside these ranges and needn't reach their ends.
All inputs are finite; a program needn't handle non-finite values.
Results may differ from the reference program's by a relative error of at most 0.03.
Values may be sent and summed in bfloat16 or wider, within the bound.
A program may use at most 64 MiB of HBM per device.

```python
import math
import jax
import jax.numpy as jnp
from jax import lax

D = 2048
FF = 7168
EXPERTS = 16
HEADS = 64
HDIM = 64
DSTATE = 128
BLOCK = 128
TOKENS = 4096
INNER = 4096
NBLK = 32
N_EXP = 16


def draw_a_log(key, part):
    first_key, second_key, third_key = jax.random.split(jax.random.fold_in(key, 11), 3)
    slow_share = 0.5
    slow_heads = jax.random.uniform(first_key, (HEADS,)) < slow_share
    fast_rate = 0.03 * jnp.exp(jax.random.uniform(second_key, (HEADS,), minval=-0.5, maxval=0.5))
    slow_rate = jnp.exp(jax.random.uniform(third_key, (HEADS,), minval=math.log(0.2), maxval=math.log(2.0))) / TOKENS
    return jnp.log(jnp.where(slow_heads, slow_rate, fast_rate)).astype(jnp.float32)


def draw_residual(key, part):
    first_key, second_key, third_key = jax.random.split(jax.random.fold_in(key, 23), 3)
    row_scale = jnp.exp(jax.random.uniform(first_key, (TOKENS, 1), minval=0.0, maxval=math.log(10.0)))
    column_place = jnp.arange(D, dtype=jnp.float32)[None, :] / D
    column_scale = jnp.exp(math.log(3.0) * column_place + jax.random.uniform(second_key, (1, D), minval=-0.3, maxval=0.3))
    base_value = jax.random.normal(third_key, (TOKENS, D))
    return (0.3 * base_value * row_scale * column_scale).astype(jnp.bfloat16)


def level_of(rng, extent, cuts, smallest, high):
    factor_of = 1.0
    for dim, blocks in cuts:
        draws = jax.random.uniform(jax.random.fold_in(jax.random.fold_in(rng, 6), dim), (blocks,), jnp.float32, smallest / len(cuts), high / len(cuts))
        factor_of = factor_of * jnp.repeat(jnp.exp(draws), extent[dim] // blocks).reshape((-1,) + (1,) * (len(extent) - 1 - dim))
    return factor_of


def different_ones(key, rows, number_of, top, lift):
    sequence = jax.random.permutation(jax.random.fold_in(key, 1), number_of)
    boost = sequence
    for power in range(3):
        boost = boost * boost // number_of
    boost = boost * lift // number_of
    chance = jax.random.randint(jax.random.fold_in(key, 2), (rows, number_of), 0, 4096) + boost
    fixed_rows = jax.random.permutation(jax.random.fold_in(key, 3), rows)[jnp.arange(number_of) % rows]
    chance = jnp.where(jnp.arange(rows)[:, None] == fixed_rows[None, :], 1 << 14, chance)
    score = chance * number_of + jnp.arange(number_of)
    return lax.top_k(score.astype(jnp.int32), top)[1].astype(jnp.int32)


def centred(own_key, shape, scale, reach, cuts=(), kind=jnp.bfloat16):
    loudness = level_of(own_key, shape, cuts, -0.22, 0.18) if cuts else 1.0
    result = jax.random.normal(own_key, shape, jnp.float32) * scale * loudness
    return jnp.minimum(jnp.maximum(result, -reach), reach).astype(kind)


def setup_inputs(seed: int = 0) -> dict:
    arg_keys = jax.random.split(jax.random.key(seed), 16)
    x_in = centred(arg_keys[0], (TOKENS, INNER), 1.0, 6.0, ((0, 32), (1, 16)))
    z_gate = centred(arg_keys[1], (TOKENS, INNER), 1.0, 6.0, ((0, 32), (1, 16)))
    b_proj = centred(arg_keys[2], (TOKENS, DSTATE), DSTATE ** -0.5, 0.5, ((0, 32),))
    c_proj = centred(arg_keys[3], (TOKENS, DSTATE), DSTATE ** -0.5, 0.5, ((0, 32),))
    dt_raw = centred(arg_keys[4], (HEADS, TOKENS), 1.0, 4.0, ((0, 16), (1, 32)), jnp.float32)
    a_log = draw_a_log(jax.random.fold_in(arg_keys[15], 71), 0)
    d_skip = jnp.clip(1.0 + 0.1 * jax.random.normal(arg_keys[6], (HEADS,), jnp.float32), 0.5, 1.5)
    out_proj = centred(arg_keys[7], (INNER, D), INNER ** -0.5, 0.09375, ((0, 16),))
    residual = draw_residual(jax.random.fold_in(arg_keys[15], 71), 0)
    norm_gain = jnp.clip(1.0 + 0.1 * jax.random.normal(arg_keys[9], (D,), jnp.float32), 0.5, 1.5)
    router = centred(arg_keys[10], (D, EXPERTS), D ** -0.5, 0.125)
    w_gate = centred(arg_keys[11], (EXPERTS, D, FF), D ** -0.5, 0.125, ((1, 32), (2, 16)))
    w_up = centred(arg_keys[12], (EXPERTS, D, FF), D ** -0.5, 0.125, ((1, 32), (2, 16)))
    w_down = centred(arg_keys[13], (EXPERTS, D, FF), FF ** -0.5, 0.0625, ((1, 32), (2, 16)))
    block_experts = different_ones(arg_keys[14], NBLK, EXPERTS, 2, 2048)
    return {"x_in": x_in, "z_gate": z_gate, "b_proj": b_proj, "c_proj": c_proj, "dt_raw": dt_raw, "a_log": a_log, "d_skip": d_skip, "out_proj": out_proj, "residual": residual, "norm_gain": norm_gain, "router": router, "w_gate": w_gate, "w_up": w_up, "w_down": w_down, "block_experts": block_experts}


highest = lax.Precision.HIGHEST
epsilon = 1e-05

def block_terms(inputs_f, steps_f, keys_f, queries_f, head_rates):
    length = inputs_f.shape[0]
    log_decay = -head_rates[:, None] * steps_f
    running = jnp.cumsum(log_decay, axis=1)
    spread = running[:, :, None] - running[:, None, :]
    lower_part = jnp.arange(length)[:, None] >= jnp.arange(length)[None, :]
    weights = jnp.where(lower_part[None], jnp.exp(jnp.minimum(spread, 0.0)), 0.0)
    scores = jnp.dot(queries_f, keys_f.T, precision=highest)
    mixing = scores[None] * weights * steps_f[:, None, :]
    inside = jnp.einsum('hls,shp->lhp', mixing, inputs_f, precision=highest)
    carry_weight = jnp.exp(running[:, -1:] - running) * steps_f
    own_state = jnp.einsum('hs,shp,sn->hpn', carry_weight, inputs_f, keys_f, precision=highest)
    return (inside, own_state, jnp.exp(running), jnp.exp(running[:, -1]))

def reference(x_in, z_gate, b_proj, c_proj, dt_raw, a_log, d_skip, out_proj, residual, norm_gain, router, w_gate, w_up, w_down, block_experts):
    head_rates = jnp.exp(a_log)
    step_sizes = jax.nn.softplus(dt_raw)
    inputs_f = x_in.astype(jnp.float32).reshape(NBLK, BLOCK, HEADS, HDIM)
    steps_f = step_sizes.reshape(HEADS, NBLK, BLOCK).transpose(1, 0, 2)
    keys_f = b_proj.astype(jnp.float32).reshape(NBLK, BLOCK, DSTATE)
    queries_f = c_proj.astype(jnp.float32).reshape(NBLK, BLOCK, DSTATE)

    def advance(carried, pieces):
        inside, own_state, entry_scale, block_decay = block_terms(pieces[0], pieces[1], pieces[2], pieces[3], head_rates)
        from_before = entry_scale.T[:, :, None] * jnp.einsum('ln,hpn->lhp', pieces[3], carried, precision=highest)
        return (block_decay[:, None, None] * carried + own_state, inside + from_before)
    start_state = jnp.zeros((HEADS, HDIM, DSTATE), jnp.float32)
    _, outputs = lax.scan(advance, start_state, (inputs_f, steps_f, keys_f, queries_f))
    outputs = outputs + d_skip[None, None, :, None] * inputs_f
    gated_rows = (outputs.reshape(TOKENS, INNER) * jax.nn.silu(z_gate.astype(jnp.float32))).astype(jnp.bfloat16)
    group_rows = INNER // N_EXP
    mixed_sum = jnp.zeros((TOKENS, D), jnp.float32)
    for group_index in range(N_EXP):
        lower_row = group_index * group_rows
        partial_sum = jnp.dot(gated_rows[:, lower_row:lower_row + group_rows], out_proj[lower_row:lower_row + group_rows], preferred_element_type=jnp.float32)
        rounded = lax.optimization_barrier(partial_sum.astype(jnp.bfloat16))
        mixed_sum = mixed_sum + rounded.astype(jnp.float32)
    stream = mixed_sum + residual.astype(jnp.float32)
    mean_square = lax.optimization_barrier(jnp.mean(stream * stream, axis=1, keepdims=True))
    normed = (stream * lax.rsqrt(mean_square + epsilon) * norm_gain).astype(jnp.bfloat16)
    logits = jnp.dot(normed, router, preferred_element_type=jnp.float32).reshape(NBLK, BLOCK, EXPERTS)
    chosen = jnp.take_along_axis(logits, block_experts[:, None, :].astype(jnp.int32), axis=2)
    mixing_gates = jax.nn.sigmoid(chosen - chosen[:, :, ::-1])

    def one_block(pieces):
        rows_in, named_pair, gate_pair = pieces
        summed = jnp.zeros((BLOCK, D), jnp.float32)
        for which_slot in range(2):
            expert_index = named_pair[which_slot]
            gate_part = jnp.dot(rows_in, w_gate[expert_index], preferred_element_type=jnp.float32)
            up_part = jnp.dot(rows_in, w_up[expert_index], preferred_element_type=jnp.float32)
            hidden = (jax.nn.silu(gate_part) * up_part).astype(jnp.bfloat16)
            down_part = lax.dot_general(hidden, w_down[expert_index], (((1,), (1,)), ((), ())), preferred_element_type=jnp.float32)
            summed = summed + gate_pair[:, which_slot:which_slot + 1] * down_part
        return summed
    expert_rows = lax.map(one_block, (normed.reshape(NBLK, BLOCK, D), block_experts, mixing_gates))
    return (stream.astype(jnp.bfloat16), expert_rows.reshape(TOKENS, D).astype(jnp.bfloat16))
```

```python
import functools

import jax
import jax.numpy as jnp
from jax import lax
from jax.experimental import pallas as pl
from jax.experimental.pallas import tpu as pltpu
from jax.sharding import PartitionSpec as P

MESH = pl.DeviceIdType.MESH
F32 = jnp.float32
BF16 = jnp.bfloat16
T = 128
epsilon = 1e-05


def mm(a, b):
    return jnp.dot(a, b, preferred_element_type=F32)


def nt(a, b):
    return lax.dot_general(a, b, (((1,), (1,)), ((), ())), preferred_element_type=F32)


def split2(v):
    hi = v.astype(BF16)
    return hi, (v - hi.astype(F32)).astype(BF16)


def split3(v):
    hi = v.astype(BF16)
    rest = v - hi.astype(F32)
    mid = rest.astype(BF16)
    return hi, mid, (rest - mid.astype(F32)).astype(BF16)


def silu(v):
    return v / (1.0 + jnp.exp(-v))


def kernel(
    nz,
    nx,
    gs,
    x_ref,
    zg_ref,
    b_ref,
    c_ref,
    dt_ref,
    al_ref,
    dk_ref,
    op_ref,
    res_ref,
    gain_ref,
    rt_ref,
    wgu_in,
    wd_in,
    be_ref,
    so_ref,
    eo_ref,
    dt8,
    wgu,
    wd,
    cmsg,
    crcv,
    gbuf,
    tmsg,
    tbuf,
    ysnd,
    yrcv,
    gt,
    rs,
    usnd,
    urcv,
    xs,
    ssnd,
    srcv,
    rp,
    hb,
    os_,
    ob,
    fsnd,
    frcv,
    wl_sem,
    ws_sem,
    wr_sem,
    cs_sem,
    cr_sem,
    as_sem,
    ar_sem,
    bs_sem,
    br_sem,
    ts_sem,
    tr_sem,
    ss_sem,
    sr_sem,
    us_sem,
    ur_sem,
    gs_sem,
    gr_sem,
    rs_sem,
    rr_sem,
    hs_sem,
    hr_sem,
    os_sem,
    or_sem,
):
    ctx = lax.axis_index("ctx")
    q = lax.axis_index("exp")
    z = lax.div(ctx, 2)
    c = lax.rem(ctx, 2)
    ng = nz // gs
    member = lax.rem(z, gs)
    group = lax.div(z, gs)
    up = 2 * lax.rem(z + 1, nz) + c
    down = 2 * lax.rem(z + nz - 1, nz) + c
    other = 2 * z + (1 - c)
    mirror = (2 * q + c, z)
    hops_up = nz // 2
    hops_down = nz - 1 - hops_up

    def remote(src, dst, send, recv, to):
        return pltpu.make_async_remote_copy(
            src_ref=src,
            dst_ref=dst,
            send_sem=send,
            recv_sem=recv,
            device_id=to,
            device_id_type=MESH,
        )

    barrier = pltpu.get_barrier_semaphore()

    def greet(to):
        pl.semaphore_signal(barrier, inc=1, device_id=to, device_id_type=MESH)

    greet((other, q))
    for o in range(1, gs):
        greet((2 * (group * gs + lax.rem(member + o, gs)) + c, q))
    for o in range(1, ng):
        greet((2 * (lax.rem(group + o, ng) * gs + member) + c, q))

    def greet_plane(o, carry):
        greet((ctx, lax.rem(q + o, nx)))
        return carry

    lax.fori_loop(1, nx, greet_plane, 0)

    @pl.when(member == gs - 1)
    def _():
        greet((up, q))

    @pl.when(member == 0)
    def _():
        greet((down, q))

    @pl.when(q != z)
    def _():
        greet(mirror)

    peers = (
        (gs + ng + nx - 2)
        + (member == gs - 1).astype(jnp.int32)
        + (member == 0).astype(jnp.int32)
        + (q != z).astype(jnp.int32)
    )
    pl.semaphore_wait(barrier, peers)

    mine = pl.ds(pl.multiple_of(c * 64, 64), 64)
    theirs = pl.ds(pl.multiple_of((1 - c) * 64, 64), 64)
    w_local = (
        pltpu.make_async_copy(wgu_in, wgu.at[:, mine, :], wl_sem.at[0]),
        pltpu.make_async_copy(wd_in, wd.at[:, mine, :], wl_sem.at[1]),
    )
    w_sent = (
        remote(wgu_in, wgu.at[:, mine, :], ws_sem.at[0], wr_sem.at[0], (other, q)),
        remote(wd_in, wd.at[:, mine, :], ws_sem.at[1], wr_sem.at[1], (other, q)),
    )
    for copy in (*w_sent, *w_local):
        copy.start()

    lane = lax.broadcasted_iota(jnp.int32, (T, T), 1)
    row = lax.broadcasted_iota(jnp.int32, (T, T), 0)
    left = lane < 64
    upper = row < 64
    row8 = lax.broadcasted_iota(jnp.int32, (8, T), 0)
    dt8[...] = jnp.zeros((8, T), F32)
    dt8[0:4, :] = dt_ref[...]
    steps = jnp.log(1.0 + jnp.exp(dt8[...]))
    rate = jnp.zeros((8, T), F32)
    for h in range(4):
        rate = jnp.where(row8 == h, jnp.exp(jnp.full((8, T), al_ref[h], F32)), rate)
    log_decay = -rate * steps
    before = jnp.where(row <= lane, 1.0, 0.0).astype(BF16)
    ones = jnp.ones((T, T), BF16)
    parts = split3(log_decay)
    running = mm(parts[0], before) + (mm(parts[1], before) + mm(parts[2], before))
    totals = mm(parts[0], ones) + (mm(parts[1], ones) + mm(parts[2], ones))
    carry_w = jnp.exp(totals - running) * steps
    turned = jnp.concatenate([running, carry_w, jnp.zeros((T - 16, T), F32)], axis=0).T
    scores = nt(c_ref[...], b_ref[...])
    inside = []
    states = []
    row16 = lax.broadcasted_iota(jnp.int32, (16, T), 0)

    def log_rows(a0, a1):
        h0, l0 = split2(a0)
        h1, l1 = split2(a1)
        return jnp.where(
            row16 == 0,
            h0.astype(F32),
            jnp.where(
                row16 == 1,
                l0.astype(F32),
                jnp.where(
                    row16 == 2,
                    h1.astype(F32),
                    jnp.where(row16 == 3, l1.astype(F32), 0.0),
                ),
            ),
        ).astype(BF16)

    def unpack(message):
        tail = message[T : T + 16, :].astype(F32)
        return message[0:T, :].astype(F32), tail[0:1] + tail[1:2], tail[2:3] + tail[3:4]

    def spread(a0, a1):
        return jnp.where(upper, jnp.exp(a0), jnp.exp(a1))

    for p in range(2):
        xp = x_ref[:, p * T : (p + 1) * T]
        halves = []
        for h in (2 * p, 2 * p + 1):
            gap = turned[:, h : h + 1] - running[h : h + 1, :]
            weight = jnp.exp(jnp.minimum(gap, 0.0)) * steps[h : h + 1, :]
            hi, lo = split2(jnp.where(row >= lane, scores * weight, 0.0))
            halves.append(mm(hi, xp) + mm(lo, xp))
        inside.append(jnp.where(left, halves[0], halves[1]))
        scale = jnp.where(
            left, turned[:, 8 + 2 * p : 9 + 2 * p], turned[:, 9 + 2 * p : 10 + 2 * p]
        )
        hi, lo = split2((xp.astype(F32) * scale).T)
        states.append(mm(hi, b_ref[...]) + mm(lo, b_ref[...]))

    give = jnp.where(c == 0, states[1], states[0])
    keep = jnp.where(c == 0, states[0], states[1])
    a_pairs = [(totals[2 * p : 2 * p + 1, :], totals[2 * p + 1 : 2 * p + 2, :]) for p in range(2)]
    cmsg[0:T, :] = give.astype(BF16)
    cmsg[T : T + 16, :] = log_rows(
        jnp.where(c == 0, a_pairs[1][0], a_pairs[0][0]),
        jnp.where(c == 0, a_pairs[1][1], a_pairs[0][1]),
    )
    to_core = remote(cmsg, crcv, cs_sem.at[0], cr_sem.at[0], (other, q))
    to_core.start()
    own_a0 = jnp.where(c == 0, a_pairs[0][0], a_pairs[1][0])
    own_a1 = jnp.where(c == 0, a_pairs[0][1], a_pairs[1][1])
    to_core.wait_recv()
    got, got_a0, got_a1 = unpack(crcv)
    first = jnp.where(c == 0, keep, got)
    second = jnp.where(c == 0, got, keep)
    first_a0 = jnp.where(c == 0, own_a0, got_a0)
    first_a1 = jnp.where(c == 0, own_a1, got_a1)
    second_a0 = jnp.where(c == 0, got_a0, own_a0)
    second_a1 = jnp.where(c == 0, got_a1, own_a1)
    gbuf[member, 0:T, :] = (spread(second_a0, second_a1) * first + second).astype(BF16)
    gbuf[member, T : T + 16, :] = log_rows(first_a0 + second_a0, first_a1 + second_a1)

    def to_member(o):
        to = 2 * (group * gs + lax.rem(member + o, gs)) + c
        return remote(gbuf.at[member], gbuf.at[member], as_sem.at[o], ar_sem.at[o], (to, q))

    for o in range(1, gs):
        to_member(o).start()
    for o in range(1, gs):
        to_member(o).wait_recv()
    zero = jnp.zeros((T, T), F32)
    zero_row = jnp.zeros((1, T), F32)
    total, total_a0, total_a1 = zero, zero_row, zero_row
    part, part_a0, part_a1 = zero, zero_row, zero_row
    for m in range(gs):
        s, a0, a1 = unpack(gbuf.at[m])
        decay = spread(a0, a1)
        total, total_a0, total_a1 = decay * total + s, total_a0 + a0, total_a1 + a1
        earlier = m < member
        part = jnp.where(earlier, decay * part + s, part)
        part_a0 = jnp.where(earlier, part_a0 + a0, part_a0)
        part_a1 = jnp.where(earlier, part_a1 + a1, part_a1)
    tmsg[0:T, :] = total.astype(BF16)
    tmsg[T : T + 16, :] = log_rows(total_a0, total_a1)

    def to_group(o):
        to = 2 * (lax.rem(group + o, ng) * gs + member) + c
        return remote(tmsg, tbuf.at[o], bs_sem.at[o], br_sem.at[o], (to, q))

    for o in range(1, ng):

        @pl.when(group + o < ng)
        def _(o=o):
            to_group(o).start()

    reach = zero
    for o in range(ng - 1, 0, -1):

        @pl.when(group >= o)
        def _(o=o):
            to_group(o).wait_recv()

        @pl.when(group < o)
        def _(o=o):
            tbuf[o] = jnp.zeros((T + 16, T), BF16)

        s, a0, a1 = unpack(tbuf.at[o])
        reach = jnp.where(group >= o, spread(a0, a1) * reach + s, zero)
    at_first = spread(part_a0, part_a1) * reach + part
    at_second = spread(first_a0, first_a1) * at_first + first
    ysnd[...] = jnp.where(c == 0, at_second, at_first).astype(BF16)
    back = remote(ysnd, yrcv, cs_sem.at[1], cr_sem.at[1], (other, q))
    back.start()
    own_in = jnp.where(c == 0, at_first, at_second).astype(BF16)
    back.wait_recv()
    got_in = yrcv[...]
    entering = (
        jnp.where(c == 0, own_in.astype(F32), got_in.astype(F32)).astype(BF16),
        jnp.where(c == 0, got_in.astype(F32), own_in.astype(F32)).astype(BF16),
    )
    gated = []
    for p in range(2):
        scale = jnp.where(
            left,
            jnp.exp(turned[:, 2 * p : 2 * p + 1]),
            jnp.exp(turned[:, 2 * p + 1 : 2 * p + 2]),
        )
        skip = jnp.where(
            left,
            jnp.full((T, T), dk_ref[2 * p], F32),
            jnp.full((T, T), dk_ref[2 * p + 1], F32),
        )
        xp = x_ref[:, p * T : (p + 1) * T].astype(F32)
        zp = zg_ref[:, p * T : (p + 1) * T].astype(F32)
        out = inside[p] + scale * nt(c_ref[...], entering[p]) + skip * xp
        gated.append((out * silu(zp)).astype(BF16))

    def tile_of(index):
        return pl.ds(pl.multiple_of(index * T, T), T)

    def project(to):
        cols = tile_of(to)
        return mm(gated[0], op_ref[0:T, cols]) + mm(gated[1], op_ref[T : 2 * T, cols])

    def send_term(o):
        to = lax.rem(q + o, nx)
        return remote(gt.at[o], rs.at[o], ts_sem.at[o], tr_sem.at[o], (ctx, to))

    def project_step(o, carry):
        gt[o] = project(lax.rem(q + o, nx)).astype(BF16)
        send_term(o).start()
        return carry

    lax.fori_loop(1, nx, project_step, 0)
    own_term = project(q).astype(BF16).astype(F32)
    stream = own_term + res_ref[:, tile_of(q)].astype(F32)

    def sum_step(o, acc):
        send_term(o).wait_recv()
        return acc + rs[o].astype(F32)

    stream = lax.fori_loop(1, nx, sum_step, stream)
    so_ref[...] = stream.astype(BF16)
    scaled = (stream * gain_ref[:, tile_of(q)]).astype(BF16)
    usnd[...] = scaled
    to_mirror = remote(usnd, urcv, us_sem.at[0], ur_sem.at[0], mirror)

    @pl.when(q != z)
    def _():
        to_mirror.start()

    logits = mm(scaled, rt_ref[tile_of(q), :])
    expert = lax.broadcasted_iota(jnp.int32, (T, rt_ref.shape[1]), 1)
    chosen = jnp.where(expert == be_ref[ctx, 0], logits, 0.0)
    refused = jnp.where(expert == be_ref[ctx, 1], logits, 0.0)
    difference = jnp.sum(chosen - refused, axis=1, keepdims=True)
    square = jnp.sum(stream * stream, axis=1, keepdims=True)
    columns = jnp.where(lane == 0, square, jnp.where(lane == 1, difference, 0.0))
    ssnd[...] = columns.T[0:8, :]

    def send_stat(o):
        return remote(
            ssnd, srcv.at[o], ss_sem.at[o], sr_sem.at[o], (ctx, lax.rem(q + o, nx))
        )

    def stat_step(o, carry):
        send_stat(o).start()
        return carry

    lax.fori_loop(1, nx, stat_step, 0)

    @pl.when(q != z)
    def _():
        to_mirror.wait_recv()
        xs[q] = urcv[...]

    @pl.when(q == z)
    def _():
        xs[q] = usnd[...]

    def send_rows(o):
        to = lax.rem(q + o, nx)
        return remote(xs.at[q], xs.at[q], gs_sem.at[o], gr_sem.at[o], (ctx, to))

    def rows_step(o, carry):
        send_rows(o).start()
        return carry

    lax.fori_loop(1, nx, rows_step, 0)

    def rows_wait(o, carry):
        send_rows(o).wait_recv()
        return carry

    for copy in w_local:
        copy.wait()
    for i in range(2):
        w_sent[i].wait_recv()
    lax.fori_loop(1, nx, rows_wait, 0)

    def partial(d, k):
        return mm(xs[d], wgu[be_ref[2 * d + c, k]])

    def target(way, s):
        if way == 0:
            return lax.rem(z + hops_up - s + nz, nz)
        return lax.rem(z + nz - hops_down + s, nz)

    def send_sum(way, s, k):
        return remote(
            rp.at[way, s, k],
            rp.at[way, s + 1, k],
            rs_sem.at[way, s, k],
            rr_sem.at[way, s, k],
            ((up, down)[way], q),
        )

    ways = tuple(w for w in range(2) if (hops_up, hops_down)[w])
    for k in range(2):
        for way in ways:
            rp[way, 0, k] = partial(target(way, 0), k).astype(BF16)
            send_sum(way, 0, k).start()

    def sum_hop(way, s, k):
        value = partial(target(way, s), k)
        send_sum(way, s - 1, k).wait_recv()
        rp[way, s, k] = (value + rp[way, s, k].astype(F32)).astype(BF16)
        send_sum(way, s, k).start()

    def hop(s, carry):
        for k in range(2):
            for way in range(2):
                sum_hop(way, s, k)
        return carry

    lax.fori_loop(1, hops_down, hop, 0)
    for s in range(max(hops_down, 1), hops_up):
        for k in range(2):
            sum_hop(0, s, k)

    def stat_sum(o, acc):
        send_stat(o).wait_recv()
        return acc + srcv[o]

    stats = lax.fori_loop(1, nx, stat_sum, ssnd[...])
    inverse = lax.rsqrt(stats[0:1, :] * (1.0 / (nx * T)) + epsilon)
    gate0 = 1.0 / (1.0 + jnp.exp(-stats[1:2, :] * inverse))
    gate1 = 1.0 / (1.0 + jnp.exp(stats[1:2, :] * inverse))
    pick = jnp.where(row == 0, inverse, jnp.where(row == 1, gate0, jnp.where(row == 2, gate1, 0.0)))
    turned2 = pick.T
    norm = turned2[:, 0:1]
    rests = []
    for k in range(2):
        value = partial(z, k)
        for way in ways:
            send_sum(way, (hops_up, hops_down)[way] - 1, k).wait_recv()
            value = value + rp[way, (hops_up, hops_down)[way], k].astype(F32)
        value = value * norm
        mix = turned2[:, 1 + k : 2 + k]
        gate_main = value[:, 0:384]
        up_main = value[:, 384:768]
        both = value[:, 768:896]
        hb[z, :, 384 * k : 384 * (k + 1)] = (silu(gate_main) * up_main * mix).astype(BF16)
        swapped = pltpu.roll(both, 64, 1)
        if k == 0:
            rests.append(silu(both) * swapped * mix)
        else:
            rests.append(silu(swapped) * both * mix)
    hb[z, :, 768:896] = jnp.where(left, rests[0], rests[1]).astype(BF16)

    def send_hidden(way, s, part):
        source = lax.rem(z - s + nz, nz) if way == 0 else lax.rem(z + s, nz)
        half = hb.at[source, pl.ds(part * 64, 64), :]
        return remote(
            half,
            half,
            hs_sem.at[way, s, part],
            hr_sem.at[way, s, part],
            ((up, down)[way], q),
        )

    def arrived(way, s, part):
        source = lax.rem(z - 1 - s + nz, nz) if way == 0 else lax.rem(z + 1 + s, nz)
        half = hb.at[source, pl.ds(part * 64, 64), :]
        return remote(
            half,
            half,
            hs_sem.at[way, s, part],
            hr_sem.at[way, s, part],
            ((up, down)[way], q),
        )

    def send_out(d):
        return remote(os_.at[d], ob.at[q], os_sem.at[d], or_sem.at[q], (ctx, d))

    def finish(d):
        e0 = be_ref[2 * d + c, 0]
        e1 = be_ref[2 * d + c, 1]
        w0 = wd[e0]
        w1 = wd[e1]
        rest = jnp.where(left, w0[:, 384:512].astype(F32), w1[:, 384:512].astype(F32)).astype(BF16)
        value = (
            nt(hb[d, :, 0:384], w0[:, 0:384])
            + nt(hb[d, :, 384:768], w1[:, 0:384])
            + nt(hb[d, :, 768:896], rest)
        )
        os_[d] = value.astype(BF16)

        @pl.when(d != q)
        def _():
            send_out(d).start()

    for part in range(2):
        for way in ways:
            send_hidden(way, 0, part).start()
    finish(z)

    def pass_on(s, carry):
        for part in range(2):
            for way in range(2):
                arrived(way, s, part).wait_recv()
                send_hidden(way, s + 1, part).start()
        finish(lax.rem(z - 1 - s + nz, nz))
        finish(lax.rem(z + 1 + s, nz))
        return carry

    lax.fori_loop(0, hops_down - 1, pass_on, 0)
    for s in range(max(hops_down - 1, 0), hops_up):
        for part in range(2):
            for way in ways:
                if s < (hops_up, hops_down)[way]:
                    arrived(way, s, part).wait_recv()
                if s + 1 < (hops_up, hops_down)[way]:
                    send_hidden(way, s + 1, part).start()
        for way in ways:
            if s < (hops_up, hops_down)[way]:
                finish(lax.rem(z - 1 - s + nz, nz) if way == 0 else lax.rem(z + 1 + s, nz))

    def out_sum(o, acc):
        source = lax.rem(q + o, nx)
        remote(os_.at[q], ob.at[source], os_sem.at[q], or_sem.at[source], (ctx, source)).wait_recv()
        return acc + ob[source].astype(F32)

    result = lax.fori_loop(1, nx, out_sum, os_[q].astype(F32)).astype(BF16)
    fsnd[...] = result
    to_owner = remote(fsnd, frcv, us_sem.at[1], ur_sem.at[1], mirror)

    @pl.when(q != z)
    def _():
        to_owner.start()
        to_owner.wait_recv()
        eo_ref[...] = frcv[...]

    @pl.when(q == z)
    def _():
        eo_ref[...] = fsnd[...]

    for copy in (*w_sent, to_core, back):
        copy.wait_send()
    for o in range(1, gs):
        to_member(o).wait_send()
    for o in range(1, ng):

        @pl.when(group + o < ng)
        def _(o=o):
            to_group(o).wait_send()

    @pl.when(q != z)
    def _():
        to_mirror.wait_send()
        to_owner.wait_send()

    def drain(o, carry):
        send_term(o).wait_send()
        send_stat(o).wait_send()
        send_rows(o).wait_send()
        send_out(lax.rem(q + o, nx)).wait_send()
        return carry

    lax.fori_loop(1, nx, drain, 0)

    def drain_up(s, carry):
        for k in range(2):
            send_sum(0, s, k).wait_send()
            send_hidden(0, s, k).wait_send()
        return carry

    def drain_down(s, carry):
        for k in range(2):
            send_sum(1, s, k).wait_send()
            send_hidden(1, s, k).wait_send()
        return carry

    lax.fori_loop(0, hops_up, drain_up, 0)
    lax.fori_loop(0, hops_down, drain_down, 0)


def per_device(
    nz,
    nx,
    gs,
    x_in,
    z_gate,
    b_proj,
    c_proj,
    dt_raw,
    a_log,
    d_skip,
    out_proj,
    residual,
    norm_gain,
    router,
    w_gate,
    w_up,
    w_down,
    block_experts,
):
    experts = w_gate.shape[0]
    wide = 896
    wgu = jnp.concatenate(
        [w_gate[..., :384], w_up[..., :384], w_gate[..., 384:], w_up[..., 384:]], axis=-1
    )
    wd = jnp.concatenate([w_down, w_down[..., 384:]], axis=-1)
    vmem = pl.BlockSpec(memory_space=pltpu.VMEM)
    smem = pl.BlockSpec(memory_space=pltpu.SMEM)
    hbm = pl.BlockSpec(memory_space=pl.ANY)
    dma = pltpu.SemaphoreType.DMA
    hops = nz // 2
    tile = jax.ShapeDtypeStruct((T, T), BF16)
    return pl.pallas_call(
        functools.partial(kernel, nz, nx, gs),
        out_shape=(tile, tile),
        in_specs=[
            vmem,
            vmem,
            vmem,
            vmem,
            vmem,
            smem,
            smem,
            vmem,
            vmem,
            vmem,
            vmem,
            hbm,
            hbm,
            smem,
        ],
        out_specs=(vmem, vmem),
        scratch_shapes=[
            pltpu.VMEM((8, T), F32),
            pltpu.VMEM((experts, T, wide), BF16),
            pltpu.VMEM((experts, T, 512), BF16),
            pltpu.VMEM((T + 16, T), BF16),
            pltpu.VMEM((T + 16, T), BF16),
            pltpu.VMEM((gs, T + 16, T), BF16),
            pltpu.VMEM((T + 16, T), BF16),
            pltpu.VMEM((nz // gs, T + 16, T), BF16),
            pltpu.VMEM((T, T), BF16),
            pltpu.VMEM((T, T), BF16),
            pltpu.VMEM((nx, T, T), BF16),
            pltpu.VMEM((nx, T, T), BF16),
            pltpu.VMEM((T, T), BF16),
            pltpu.VMEM((T, T), BF16),
            pltpu.VMEM((nx, T, T), BF16),
            pltpu.VMEM((8, T), F32),
            pltpu.VMEM((nx, 8, T), F32),
            pltpu.VMEM((2, hops + 1, 2, T, wide), BF16),
            pltpu.VMEM((nz, T, wide), BF16),
            pltpu.VMEM((nx, T, T), BF16),
            pltpu.VMEM((nx, T, T), BF16),
            pltpu.VMEM((T, T), BF16),
            pltpu.VMEM((T, T), BF16),
            dma((2,)),
            dma((2,)),
            dma((2,)),
            dma((2,)),
            dma((2,)),
            dma((gs,)),
            dma((gs,)),
            dma((nz // gs,)),
            dma((nz // gs,)),
            dma((nx,)),
            dma((nx,)),
            dma((nx,)),
            dma((nx,)),
            dma((2,)),
            dma((2,)),
            dma((nx,)),
            dma((nx,)),
            dma((2, hops, 2)),
            dma((2, hops, 2)),
            dma((2, hops, 2)),
            dma((2, hops, 2)),
            dma((nx,)),
            dma((nx,)),
        ],
        compiler_params=pltpu.CompilerParams(
            collective_id=0, has_side_effects=True, vmem_limit_bytes=48 * 2**20
        ),
    )(
        x_in,
        z_gate,
        b_proj,
        c_proj,
        dt_raw,
        a_log,
        d_skip,
        out_proj,
        residual,
        norm_gain.reshape(1, -1),
        router,
        wgu,
        wd,
        block_experts,
    )


def solution(mesh):
    nz = mesh.shape["ctx"] // 2
    nx = mesh.shape["exp"]
    gs = 4 if nz >= 16 else 2
    placed = (
        P("ctx", "exp"),
        P("ctx", "exp"),
        P("ctx", None),
        P("ctx", None),
        P("exp", "ctx"),
        P("exp"),
        P("exp"),
        P("exp", None),
        P("ctx", None),
        P(),
        P(),
        P(None, "ctx", "exp"),
        P(None, "ctx", "exp"),
        P(None, "ctx", "exp"),
        P(),
    )
    return jax.shard_map(
        functools.partial(per_device, nz, nx, gs),
        mesh=mesh,
        in_specs=placed,
        out_specs=(P("ctx", "exp"), P("ctx", "exp")),
        check_vma=False,
    )
```

```python
import functools

import jax
import jax.numpy as jnp
from jax import lax
from jax.experimental import pallas as pl
from jax.experimental.pallas import tpu as pltpu
from jax.sharding import PartitionSpec as P

MESH = pl.DeviceIdType.MESH
F32 = jnp.float32
BF16 = jnp.bfloat16
T = 128
epsilon = 1e-05


def mm(a, b):
    return jnp.dot(a, b, preferred_element_type=F32)


def nt(a, b):
    return lax.dot_general(a, b, (((1,), (1,)), ((), ())), preferred_element_type=F32)


def split2(v):
    hi = v.astype(BF16)
    return hi, (v - hi.astype(F32)).astype(BF16)


def split3(v):
    hi = v.astype(BF16)
    rest = v - hi.astype(F32)
    mid = rest.astype(BF16)
    return hi, mid, (rest - mid.astype(F32)).astype(BF16)


def silu(v):
    return v / (1.0 + jnp.exp(-v))


def kernel(
    nz,
    nx,
    gs,
    x_in,
    zg_in,
    b_in,
    c_in,
    dt_in,
    al_ref,
    dk_ref,
    op_in,
    res_in,
    gain_in,
    rt_in,
    wg_in,
    wu_in,
    wd_in,
    be_ref,
    so_ref,
    eo_ref,
    x_ref,
    zg_ref,
    b_ref,
    c_ref,
    dt_ref,
    op_ref,
    res_ref,
    gain_ref,
    rt_ref,
    dt8,
    wg_stage,
    wu_stage,
    wd_stage,
    wgu,
    wd,
    cmsg,
    crcv,
    gbuf,
    tmsg,
    tbuf,
    ysnd,
    yrcv,
    gt,
    rs,
    usnd,
    urcv,
    xs,
    ssnd,
    srcv,
    rp,
    hb0,
    hb1,
    os_,
    ob,
    fsnd,
    frcv,
    osnd,
    orcv,
    flast,
    in_sem,
    wl_sem,
    ws_sem,
    wr_sem,
    cs_sem,
    cr_sem,
    as_sem,
    ar_sem,
    bs_sem,
    br_sem,
    ts_sem,
    tr_sem,
    ss_sem,
    sr_sem,
    us_sem,
    ur_sem,
    ps_sem,
    pr_sem,
    gs_sem,
    gr_sem,
    rs_sem,
    rr_sem,
    hs_sem,
    hr_sem,
    os_sem,
    or_sem,
):
    ctx = lax.axis_index("ctx")
    q = lax.axis_index("exp")
    z = lax.div(ctx, 2)
    c = lax.rem(ctx, 2)
    ng = nz // gs
    member = lax.rem(z, gs)
    group = lax.div(z, gs)
    up = 2 * lax.rem(z + 1, nz) + c
    down = 2 * lax.rem(z + nz - 1, nz) + c
    other = 2 * z + (1 - c)
    share = lax.rem(q - z + nx, nx)
    opposite = (2 * share + c, q)
    home = (ctx, share)
    hops_up = nz // 2
    hops_down = nz - 1 - hops_up

    def remote(src, dst, send, recv, to):
        return pltpu.make_async_remote_copy(
            src_ref=src,
            dst_ref=dst,
            send_sem=send,
            recv_sem=recv,
            device_id=to,
            device_id_type=MESH,
        )

    def tile_of(index):
        return pl.ds(pl.multiple_of(index * T, T), T)

    inputs = tuple(
        pltpu.make_async_copy(src, dst, in_sem.at[i])
        for i, (src, dst) in enumerate(
            (
                (dt_in, dt_ref),
                (b_in, b_ref),
                (c_in, c_ref),
                (x_in, x_ref),
                (zg_in, zg_ref),
                (op_in, op_ref),
                (res_in.at[:, tile_of(share)], res_ref),
                (gain_in.at[:, tile_of(share)], gain_ref),
                (rt_in.at[:, tile_of(share)], rt_ref),
            )
        )
    )
    for copy in inputs:
        copy.start()

    barrier = pltpu.get_barrier_semaphore()

    def greet(to):
        pl.semaphore_signal(barrier, inc=1, device_id=to, device_id_type=MESH)

    greet((other, q))
    for o in range(1, gs):
        greet((2 * (group * gs + lax.rem(member + o, gs)) + c, q))
    for o in range(1, ng):
        greet((2 * (lax.rem(group + o, ng) * gs + member) + c, q))

    def greet_plane(o, carry):
        greet((ctx, lax.rem(q + o, nx)))
        return carry

    lax.fori_loop(1, nx, greet_plane, 0)

    @pl.when(member == gs - 1)
    def _():
        greet((up, q))

    @pl.when(member == 0)
    def _():
        greet((down, q))

    share_up = jnp.logical_and(member == gs - 1, 2 * share + c == up)
    share_down = jnp.logical_and(member == 0, 2 * share + c == down)
    near = jnp.logical_or(lax.div(share, gs) == group, lax.rem(share, gs) == member)
    apart = jnp.logical_not(jnp.logical_or(near, jnp.logical_or(share_up, share_down)))

    @pl.when(apart)
    def _():
        greet(opposite)

    peers = (
        (gs + ng + nx - 2)
        + (member == gs - 1).astype(jnp.int32)
        + (member == 0).astype(jnp.int32)
        + apart.astype(jnp.int32)
    )

    mine = pl.ds(pl.multiple_of(c * 64, 64), 64)
    w_local = tuple(
        pltpu.make_async_copy(src, dst, wl_sem.at[i])
        for i, (src, dst) in enumerate(((wg_in, wg_stage), (wu_in, wu_stage), (wd_in, wd_stage)))
    )
    w_sent = tuple(
        remote(w.at[:, mine, :], w.at[:, mine, :], ws_sem.at[i], wr_sem.at[i], (other, q))
        for i, w in enumerate((wgu, wd))
    )

    def pack(e, carry):
        gate, rise, fall = wg_stage[e], wu_stage[e], wd_stage[e]
        wgu[e, mine, 0:384] = gate[:, 0:384]
        wgu[e, mine, 384:768] = rise[:, 0:384]
        wgu[e, mine, 768:896] = jnp.concatenate([gate[:, 384:448], rise[:, 384:448]], axis=1)
        wd[e, mine, 0:384] = fall[:, 0:384]
        wd[e, mine, 384:512] = jnp.concatenate([fall[:, 384:448], fall[:, 384:448]], axis=1)
        return carry

    for copy in w_local:
        copy.start()
    for copy in inputs[0:4]:
        copy.wait()

    lane = lax.broadcasted_iota(jnp.int32, (T, T), 1)
    row = lax.broadcasted_iota(jnp.int32, (T, T), 0)
    left = lane < 64
    upper = row < 64
    row8 = lax.broadcasted_iota(jnp.int32, (8, T), 0)
    dt8[...] = jnp.zeros((8, T), F32)
    dt8[0:4, :] = dt_ref[...]
    steps = jnp.log(1.0 + jnp.exp(dt8[...]))
    rate = jnp.zeros((8, T), F32)
    for h in range(4):
        rate = jnp.where(row8 == h, jnp.exp(jnp.full((8, T), al_ref[h], F32)), rate)
    log_decay = -rate * steps
    before = jnp.where(row <= lane, 1.0, 0.0).astype(BF16)
    ones = jnp.ones((T, T), BF16)
    parts = split3(log_decay)
    running = mm(parts[0], before) + (mm(parts[1], before) + mm(parts[2], before))
    totals = mm(parts[0], ones) + (mm(parts[1], ones) + mm(parts[2], ones))
    carry_w = jnp.exp(totals - running) * steps
    turned = jnp.concatenate([running, carry_w, jnp.zeros((T - 16, T), F32)], axis=0).T
    scores = nt(c_ref[...], b_ref[...])
    inside = []
    states = []
    row16 = lax.broadcasted_iota(jnp.int32, (16, T), 0)

    def log_rows(a0, a1):
        h0, l0 = split2(a0)
        h1, l1 = split2(a1)
        return jnp.where(
            row16 == 0,
            h0.astype(F32),
            jnp.where(
                row16 == 1,
                l0.astype(F32),
                jnp.where(
                    row16 == 2,
                    h1.astype(F32),
                    jnp.where(row16 == 3, l1.astype(F32), 0.0),
                ),
            ),
        ).astype(BF16)

    def unpack(message):
        tail = message[T : T + 16, :].astype(F32)
        return message[0:T, :].astype(F32), tail[0:1] + tail[1:2], tail[2:3] + tail[3:4]

    def spread(a0, a1):
        return jnp.where(upper, jnp.exp(a0), jnp.exp(a1))

    for p in range(2):
        xp = x_ref[:, p * T : (p + 1) * T]
        halves = []
        for h in (2 * p, 2 * p + 1):
            gap = turned[:, h : h + 1] - running[h : h + 1, :]
            weight = jnp.exp(jnp.minimum(gap, 0.0)) * steps[h : h + 1, :]
            hi, lo = split2(jnp.where(row >= lane, scores * weight, 0.0))
            halves.append(mm(hi, xp) + mm(lo, xp))
        inside.append(jnp.where(left, halves[0], halves[1]))
        scale = jnp.where(
            left, turned[:, 8 + 2 * p : 9 + 2 * p], turned[:, 9 + 2 * p : 10 + 2 * p]
        )
        hi, lo = split2((xp.astype(F32) * scale).T)
        states.append(mm(hi, b_ref[...]) + mm(lo, b_ref[...]))

    pl.semaphore_wait(barrier, peers)

    give = jnp.where(c == 0, states[1], states[0])
    keep = jnp.where(c == 0, states[0], states[1])
    a_pairs = [(totals[2 * p : 2 * p + 1, :], totals[2 * p + 1 : 2 * p + 2, :]) for p in range(2)]
    cmsg[0:T, :] = give.astype(BF16)
    cmsg[T : T + 16, :] = log_rows(
        jnp.where(c == 0, a_pairs[1][0], a_pairs[0][0]),
        jnp.where(c == 0, a_pairs[1][1], a_pairs[0][1]),
    )
    to_core = remote(cmsg, crcv, cs_sem.at[0], cr_sem.at[0], (other, q))
    to_core.start()
    own_a0 = jnp.where(c == 0, a_pairs[0][0], a_pairs[1][0])
    own_a1 = jnp.where(c == 0, a_pairs[0][1], a_pairs[1][1])
    to_core.wait_recv()
    got, got_a0, got_a1 = unpack(crcv)
    first = jnp.where(c == 0, keep, got)
    second = jnp.where(c == 0, got, keep)
    first_a0 = jnp.where(c == 0, own_a0, got_a0)
    first_a1 = jnp.where(c == 0, own_a1, got_a1)
    second_a0 = jnp.where(c == 0, got_a0, own_a0)
    second_a1 = jnp.where(c == 0, got_a1, own_a1)
    gbuf[member, 0:T, :] = (spread(second_a0, second_a1) * first + second).astype(BF16)
    gbuf[member, T : T + 16, :] = log_rows(first_a0 + second_a0, first_a1 + second_a1)

    def to_member(o):
        to = 2 * (group * gs + lax.rem(member + o, gs)) + c
        return remote(gbuf.at[member], gbuf.at[member], as_sem.at[o], ar_sem.at[o], (to, q))

    for o in range(1, gs):
        to_member(o).start()
    for copy in w_local:
        copy.wait()
    lax.fori_loop(0, wg_in.shape[0], pack, 0)
    for o in range(1, gs):
        to_member(o).wait_recv()
    zero = jnp.zeros((T, T), F32)
    zero_row = jnp.zeros((1, T), F32)
    total, total_a0, total_a1 = zero, zero_row, zero_row
    part, part_a0, part_a1 = zero, zero_row, zero_row
    for m in range(gs):
        s, a0, a1 = unpack(gbuf.at[m])
        decay = spread(a0, a1)
        total, total_a0, total_a1 = decay * total + s, total_a0 + a0, total_a1 + a1
        earlier = m < member
        part = jnp.where(earlier, decay * part + s, part)
        part_a0 = jnp.where(earlier, part_a0 + a0, part_a0)
        part_a1 = jnp.where(earlier, part_a1 + a1, part_a1)
    tmsg[0:T, :] = total.astype(BF16)
    tmsg[T : T + 16, :] = log_rows(total_a0, total_a1)

    def to_group(o):
        to = 2 * (lax.rem(group + o, ng) * gs + member) + c
        return remote(tmsg, tbuf.at[o], bs_sem.at[o], br_sem.at[o], (to, q))

    for o in range(1, ng):

        @pl.when(group + o < ng)
        def _(o=o):
            to_group(o).start()

    reach = zero
    for o in range(ng - 1, 0, -1):

        @pl.when(group >= o)
        def _(o=o):
            to_group(o).wait_recv()

        @pl.when(group < o)
        def _(o=o):
            tbuf[o] = jnp.zeros((T + 16, T), BF16)

        s, a0, a1 = unpack(tbuf.at[o])
        reach = jnp.where(group >= o, spread(a0, a1) * reach + s, zero)
    at_first = spread(part_a0, part_a1) * reach + part
    at_second = spread(first_a0, first_a1) * at_first + first
    ysnd[...] = jnp.where(c == 0, at_second, at_first).astype(BF16)
    back = remote(ysnd, yrcv, cs_sem.at[1], cr_sem.at[1], (other, q))
    back.start()
    for copy in w_sent:
        copy.start()
    own_in = jnp.where(c == 0, at_first, at_second).astype(BF16)
    back.wait_recv()
    got_in = yrcv[...]
    entering = (
        jnp.where(c == 0, own_in.astype(F32), got_in.astype(F32)).astype(BF16),
        jnp.where(c == 0, got_in.astype(F32), own_in.astype(F32)).astype(BF16),
    )
    for copy in inputs[4:]:
        copy.wait()
    gated = []
    for p in range(2):
        scale = jnp.where(
            left,
            jnp.exp(turned[:, 2 * p : 2 * p + 1]),
            jnp.exp(turned[:, 2 * p + 1 : 2 * p + 2]),
        )
        skip = jnp.where(
            left,
            jnp.full((T, T), dk_ref[2 * p], F32),
            jnp.full((T, T), dk_ref[2 * p + 1], F32),
        )
        xp = x_ref[:, p * T : (p + 1) * T].astype(F32)
        zp = zg_ref[:, p * T : (p + 1) * T].astype(F32)
        out = inside[p] + scale * nt(c_ref[...], entering[p]) + skip * xp
        gated.append((out * silu(zp)).astype(BF16))

    def project(to):
        cols = tile_of(lax.rem(to - z + nx, nx))
        return mm(gated[0], op_ref[0:T, cols]) + mm(gated[1], op_ref[T : 2 * T, cols])

    def send_term(o):
        to = lax.rem(q + o, nx)
        return remote(gt.at[o], rs.at[o], ts_sem.at[o], tr_sem.at[o], (ctx, to))

    def project_step(o, carry):
        gt[o] = project(lax.rem(q + o, nx)).astype(BF16)
        send_term(o).start()
        return carry

    lax.fori_loop(1, nx, project_step, 0)
    own_term = project(q).astype(BF16).astype(F32)
    stream = own_term + res_ref[...].astype(F32)

    def sum_step(o, acc):
        send_term(o).wait_recv()
        return acc + rs[o].astype(F32)

    stream = lax.fori_loop(1, nx, sum_step, stream)
    scaled = (stream * gain_ref[...]).astype(BF16)
    usnd[...] = scaled
    to_opposite = remote(usnd, urcv, us_sem.at[0], ur_sem.at[0], opposite)

    @pl.when(share != z)
    def _():
        to_opposite.start()

    osnd[...] = stream.astype(BF16)
    stream_home = remote(osnd, orcv, ps_sem.at[0], pr_sem.at[0], home)

    @pl.when(share != q)
    def _():
        stream_home.start()

    logits = nt(scaled, rt_ref[...])
    expert = lax.broadcasted_iota(jnp.int32, (T, rt_ref.shape[0]), 1)
    chosen = jnp.where(expert == be_ref[0, ctx], logits, 0.0)
    refused = jnp.where(expert == be_ref[1, ctx], logits, 0.0)
    difference = jnp.sum(chosen - refused, axis=1, keepdims=True)
    square = jnp.sum(stream * stream, axis=1, keepdims=True)
    columns = jnp.where(lane == 0, square, jnp.where(lane == 1, difference, 0.0))
    ssnd[...] = columns.T[0:8, :]

    def send_stat(o):
        return remote(
            ssnd, srcv.at[o], ss_sem.at[o], sr_sem.at[o], (ctx, lax.rem(q + o, nx))
        )

    def stat_step(o, carry):
        send_stat(o).start()
        return carry

    lax.fori_loop(1, nx, stat_step, 0)

    @pl.when(share != z)
    def _():
        to_opposite.wait_recv()
        xs[share] = urcv[...]

    @pl.when(share == z)
    def _():
        xs[share] = usnd[...]

    def send_rows(o):
        to = lax.rem(q + o, nx)
        return remote(xs.at[share], xs.at[share], gs_sem.at[o], gr_sem.at[o], (ctx, to))

    def rows_step(o, carry):
        send_rows(o).start()
        return carry

    lax.fori_loop(1, nx, rows_step, 0)

    def rows_ready(d):
        source = lax.rem(d + z, nx)
        o = lax.rem(q - source + nx, nx)

        @pl.when(o != 0)
        def _():
            remote(xs.at[d], xs.at[d], gs_sem.at[o], gr_sem.at[o], (ctx, source)).wait_recv()

    for copy in w_sent:
        copy.wait_recv()

    def partial(d, k):
        return mm(xs[d], wgu[be_ref[k, 2 * d + c]])

    hops = (hops_up, hops_down)

    def goes_up(way, k):
        return (way == 0) == (k == 0)

    def target(way, s, k):
        if goes_up(way, k):
            return lax.rem(z + hops[way] - s + nz, nz)
        return lax.rem(z + nz - hops[way] + s, nz)

    def send_sum(way, s, k):
        return remote(
            rp.at[way, s, k],
            rp.at[way, s + 1, k],
            rs_sem.at[way, s, k],
            rr_sem.at[way, s, k],
            (up if goes_up(way, k) else down, q),
        )

    rows_ready(lax.rem(z + hops_up, nz))
    for far in (1, nz - 1):
        rows_ready(lax.rem(z + hops_up + far, nz))
    for k in range(2):
        for way in range(2):
            rp[way, 0, k] = partial(target(way, 0, k), k).astype(BF16)
            send_sum(way, 0, k).start()

    def sum_hop(way, s, k):
        value = partial(target(way, s, k), k)
        send_sum(way, s - 1, k).wait_recv()
        rp[way, s, k] = (value + rp[way, s, k].astype(F32)).astype(BF16)
        send_sum(way, s, k).start()

    def hop(s, carry):
        rows_ready(lax.rem(z + hops_up + 1 + s, nz))
        rows_ready(lax.rem(z + hops_up - 1 - s + nz, nz))
        for k in range(2):
            for way in range(2):
                sum_hop(way, s, k)
        return carry

    lax.fori_loop(1, hops_down, hop, 0)
    for k in range(2):
        sum_hop(0, hops_down, k)
    rows_ready(z)

    def stat_sum(o, acc):
        send_stat(o).wait_recv()
        return acc + srcv[o]

    stats = lax.fori_loop(1, nx, stat_sum, ssnd[...])
    inverse = lax.rsqrt(stats[0:1, :] * (1.0 / (nx * T)) + epsilon)
    gate0 = 1.0 / (1.0 + jnp.exp(-stats[1:2, :] * inverse))
    gate1 = 1.0 / (1.0 + jnp.exp(stats[1:2, :] * inverse))
    pick = jnp.where(row == 0, inverse, jnp.where(row == 1, gate0, jnp.where(row == 2, gate1, 0.0)))
    turned2 = pick.T
    norm = turned2[:, 0:1]
    hb = (hb0, hb1)

    def source_of(way, s, k):
        return lax.rem(z - s + nz, nz) if goes_up(way, k) else lax.rem(z + s, nz)

    def pass_hidden(way, s, k, source):
        return remote(
            hb[k].at[source],
            hb[k].at[source],
            hs_sem.at[way, s, k],
            hr_sem.at[way, s, k],
            (up if goes_up(way, k) else down, q),
        )

    def send_hidden(way, s, k):
        return pass_hidden(way, s, k, source_of(way, s, k))

    def arrived(way, s, k):
        return pass_hidden(way, s, k, source_of(way, s + 1, k))

    rest0 = None
    own = (partial(z, 0), partial(z, 1))
    for k in range(2):
        value = own[k]
        for way in (1, 0):
            send_sum(way, hops[way] - 1, k).wait_recv()
            value = value + rp[way, hops[way], k].astype(F32)
        value = value * norm
        mix = turned2[:, 1 + k : 2 + k]
        both = value[:, 768:896]
        swapped = pltpu.roll(both, 64, 1)
        main = (silu(value[:, 0:384]) * value[:, 384:768] * mix).astype(BF16)
        if k == 0:
            rest0 = silu(both) * swapped * mix
            hb0[z] = main
        else:
            hb1[z, :, 0:384] = main
            hb1[z, :, 384:512] = jnp.where(left, rest0, silu(swapped) * both * mix).astype(BF16)
        for way in range(2):
            send_hidden(way, 0, k).start()

    def send_out(d):
        to = lax.rem(d + z, nx)
        return remote(os_.at[d], ob.at[q], os_sem.at[d], or_sem.at[q], (ctx, to))

    def finish(d):
        e0 = be_ref[0, 2 * d + c]
        e1 = be_ref[1, 2 * d + c]
        w0 = wd[e0]
        w1 = wd[e1]
        rest = jnp.where(left, w0[:, 384:512].astype(F32), w1[:, 384:512].astype(F32)).astype(BF16)
        value = (
            nt(hb0[d], w0[:, 0:384])
            + nt(hb1[d, :, 0:384], w1[:, 0:384])
            + nt(hb1[d, :, 384:512], rest)
        )
        os_[d] = value.astype(BF16)

        @pl.when(d != share)
        def _():
            send_out(d).start()

    def pass_on(s, first, both):
        for k in range(2):
            arrived(0, s, k).wait_recv()
            send_hidden(0, s + 1, k).start()
            arrived(1, s, k).wait_recv()
            if both:
                send_hidden(1, s + 1, k).start()
            if not first:
                finish(lax.rem(z - s + nz, nz) if k == 0 else lax.rem(z + s, nz))
            elif k == 0:
                finish(z)

    def pass_step(s, carry):
        pass_on(s, False, True)
        return carry

    pass_on(0, True, hops_down > 1)
    if hops_down > 1:
        lax.fori_loop(1, hops_down - 1, pass_step, 0)
        pass_on(hops_down - 1, False, False)
    finish(lax.rem(z - hops_down + nz, nz))
    finish(lax.rem(z + hops_down, nz))
    for k in range(2):
        arrived(0, hops_down, k).wait_recv()
    finish(lax.rem(z + hops_up, nz))

    def out_sum(o, acc):
        source = lax.rem(q + o, nx)
        remote(os_.at[0], ob.at[source], os_sem.at[0], or_sem.at[source], (ctx, source)).wait_recv()
        return acc + ob[source].astype(F32)

    fsnd[...] = lax.fori_loop(1, nx, out_sum, os_[share].astype(F32)).astype(BF16)
    to_owner = remote(fsnd, frcv, us_sem.at[1], ur_sem.at[1], opposite)
    owner_home = remote(frcv, flast, ps_sem.at[1], pr_sem.at[1], home)

    @pl.when(share != z)
    def _():
        to_owner.start()
        to_owner.wait_recv()

    @pl.when(share == z)
    def _():
        frcv[...] = fsnd[...]

    @pl.when(share != q)
    def _():
        owner_home.start()
        stream_home.wait_recv()
        so_ref[...] = orcv[...]
        owner_home.wait_recv()
        eo_ref[...] = flast[...]

    @pl.when(share == q)
    def _():
        so_ref[...] = osnd[...]
        eo_ref[...] = frcv[...]

    for copy in (*w_sent, to_core, back):
        copy.wait_send()
    for o in range(1, gs):
        to_member(o).wait_send()
    for o in range(1, ng):

        @pl.when(group + o < ng)
        def _(o=o):
            to_group(o).wait_send()

    @pl.when(share != z)
    def _():
        to_opposite.wait_send()
        to_owner.wait_send()

    @pl.when(share != q)
    def _():
        stream_home.wait_send()
        owner_home.wait_send()

    def drain(o, carry):
        send_term(o).wait_send()
        send_stat(o).wait_send()
        send_rows(o).wait_send()
        send_out(lax.rem(share + o, nx)).wait_send()
        return carry

    lax.fori_loop(1, nx, drain, 0)

    def drain_up(s, carry):
        for k in range(2):
            send_sum(0, s, k).wait_send()
            send_hidden(0, s, k).wait_send()
        return carry

    def drain_down(s, carry):
        for k in range(2):
            send_sum(1, s, k).wait_send()
            send_hidden(1, s, k).wait_send()
        return carry

    lax.fori_loop(0, hops_up, drain_up, 0)
    lax.fori_loop(0, hops_down, drain_down, 0)


def per_device(
    nz,
    nx,
    gs,
    x_in,
    z_gate,
    b_proj,
    c_proj,
    dt_raw,
    a_log,
    d_skip,
    out_proj,
    residual,
    norm_gain,
    router,
    w_gate,
    w_up,
    w_down,
    block_experts,
):
    experts = w_gate.shape[0]
    wide = 896
    vmem = pl.BlockSpec(memory_space=pltpu.VMEM)
    smem = pl.BlockSpec(memory_space=pltpu.SMEM)
    hbm = pl.BlockSpec(memory_space=pl.ANY)
    dma = pltpu.SemaphoreType.DMA
    hops = nz // 2
    tile = jax.ShapeDtypeStruct((T, T), BF16)
    return pl.pallas_call(
        functools.partial(kernel, nz, nx, gs),
        out_shape=(tile, tile),
        in_specs=[
            hbm,
            hbm,
            hbm,
            hbm,
            hbm,
            smem,
            smem,
            hbm,
            hbm,
            hbm,
            hbm,
            hbm,
            hbm,
            hbm,
            smem,
        ],
        out_specs=(vmem, vmem),
        scratch_shapes=[
            pltpu.VMEM(x_in.shape, BF16),
            pltpu.VMEM(x_in.shape, BF16),
            pltpu.VMEM((T, T), BF16),
            pltpu.VMEM((T, T), BF16),
            pltpu.VMEM(dt_raw.shape, F32),
            pltpu.VMEM(out_proj.shape, BF16),
            pltpu.VMEM((T, T), BF16),
            pltpu.VMEM((1, T), F32),
            pltpu.VMEM((experts, T), BF16),
            pltpu.VMEM((8, T), F32),
            pltpu.VMEM(w_gate.shape, BF16),
            pltpu.VMEM(w_gate.shape, BF16),
            pltpu.VMEM(w_gate.shape, BF16),
            pltpu.VMEM((experts, T, wide), BF16),
            pltpu.VMEM((experts, T, 512), BF16),
            pltpu.VMEM((T + 16, T), BF16),
            pltpu.VMEM((T + 16, T), BF16),
            pltpu.VMEM((gs, T + 16, T), BF16),
            pltpu.VMEM((T + 16, T), BF16),
            pltpu.VMEM((nz // gs, T + 16, T), BF16),
            pltpu.VMEM((T, T), BF16),
            pltpu.VMEM((T, T), BF16),
            pltpu.VMEM((nx, T, T), BF16),
            pltpu.VMEM((nx, T, T), BF16),
            pltpu.VMEM((T, T), BF16),
            pltpu.VMEM((T, T), BF16),
            pltpu.VMEM((nx, T, T), BF16),
            pltpu.VMEM((8, T), F32),
            pltpu.VMEM((nx, 8, T), F32),
            pltpu.VMEM((2, hops + 1, 2, T, wide), BF16),
            pltpu.VMEM((nz, T, 384), BF16),
            pltpu.VMEM((nz, T, 512), BF16),
            pltpu.VMEM((nx, T, T), BF16),
            pltpu.VMEM((nx, T, T), BF16),
            pltpu.VMEM((T, T), BF16),
            pltpu.VMEM((T, T), BF16),
            pltpu.VMEM((T, T), BF16),
            pltpu.VMEM((T, T), BF16),
            pltpu.VMEM((T, T), BF16),
            dma((9,)),
            dma((3,)),
            dma((2,)),
            dma((2,)),
            dma((2,)),
            dma((2,)),
            dma((gs,)),
            dma((gs,)),
            dma((nz // gs,)),
            dma((nz // gs,)),
            dma((nx,)),
            dma((nx,)),
            dma((nx,)),
            dma((nx,)),
            dma((2,)),
            dma((2,)),
            dma((2,)),
            dma((2,)),
            dma((nx,)),
            dma((nx,)),
            dma((2, hops, 2)),
            dma((2, hops, 2)),
            dma((2, hops, 2)),
            dma((2, hops, 2)),
            dma((nx,)),
            dma((nx,)),
        ],
        compiler_params=pltpu.CompilerParams(
            collective_id=0, has_side_effects=True, vmem_limit_bytes=60 * 2**20
        ),
    )(
        x_in,
        z_gate,
        b_proj,
        c_proj,
        dt_raw,
        a_log,
        d_skip,
        out_proj,
        residual,
        norm_gain.reshape(1, -1),
        router.T,
        w_gate,
        w_up,
        w_down,
        block_experts.T,
    )


def solution(mesh):
    nz = mesh.shape["ctx"] // 2
    nx = mesh.shape["exp"]
    gs = 4 if nz >= 16 else 2
    placed = (
        P("ctx", "exp"),
        P("ctx", "exp"),
        P("ctx", None),
        P("ctx", None),
        P("exp", "ctx"),
        P("exp"),
        P("exp"),
        P("exp", None),
        P("ctx", None),
        P(),
        P(),
        P(None, "ctx", "exp"),
        P(None, "ctx", "exp"),
        P(None, "ctx", "exp"),
        P(),
    )
    return jax.shard_map(
        functools.partial(per_device, nz, nx, gs),
        mesh=mesh,
        in_specs=placed,
        out_specs=(P("ctx", "exp"), P("ctx", "exp")),
        check_vma=False,
    )
```

```python
import functools

import jax
import jax.numpy as jnp
from jax import lax
from jax.experimental import pallas as pl
from jax.experimental.pallas import tpu as pltpu
from jax.sharding import PartitionSpec as P

MESH = pl.DeviceIdType.MESH
F32 = jnp.float32
BF16 = jnp.bfloat16
T = 128
epsilon = 1e-05


def mm(a, b):
    return jnp.dot(a, b, preferred_element_type=F32)


def nt(a, b):
    return lax.dot_general(a, b, (((1,), (1,)), ((), ())), preferred_element_type=F32)


def split2(v):
    hi = v.astype(BF16)
    return hi, (v - hi.astype(F32)).astype(BF16)


def split3(v):
    hi = v.astype(BF16)
    rest = v - hi.astype(F32)
    mid = rest.astype(BF16)
    return hi, mid, (rest - mid.astype(F32)).astype(BF16)


def silu(v):
    return v / (1.0 + jnp.exp(-v))


def kernel(
    nz,
    nx,
    gs,
    x_in,
    zg_in,
    b_in,
    c_in,
    dt_in,
    al_ref,
    dk_ref,
    op_in,
    res_in,
    gain_in,
    rt_in,
    wg_in,
    wu_in,
    wd_in,
    be_ref,
    out_ref,
    x_ref,
    zg_ref,
    b_ref,
    c_ref,
    dt_ref,
    op_ref,
    res_ref,
    gain_ref,
    rt_ref,
    dt8,
    wg_stage,
    wu_stage,
    wd_stage,
    wgu,
    wd,
    cmsg,
    crcv,
    gbuf,
    tmsg,
    tbuf,
    ysnd,
    yrcv,
    gt,
    rs,
    usnd,
    urcv,
    xs,
    ssnd,
    srcv,
    rp,
    hb0,
    hb1,
    os_,
    ob,
    fsnd,
    frcv,
    osnd,
    orcv,
    in_sem,
    wl_sem,
    ws_sem,
    wr_sem,
    cs_sem,
    cr_sem,
    as_sem,
    ar_sem,
    bs_sem,
    br_sem,
    ts_sem,
    tr_sem,
    ss_sem,
    sr_sem,
    us_sem,
    ur_sem,
    ps_sem,
    pr_sem,
    gs_sem,
    gr_sem,
    rs_sem,
    rr_sem,
    hs_sem,
    hr_sem,
    os_sem,
    or_sem,
):
    ctx = lax.axis_index("ctx")
    q = lax.axis_index("exp")
    z = lax.div(ctx, 2)
    c = lax.rem(ctx, 2)
    ng = nz // gs
    member = lax.rem(z, gs)
    group = lax.div(z, gs)
    up = 2 * lax.rem(z + 1, nz) + c
    down = 2 * lax.rem(z + nz - 1, nz) + c
    other = 2 * z + (1 - c)
    share = lax.rem(q - z + nx, nx)
    opposite = (2 * share + c, q)
    home = (ctx, share)
    hops_up = nz // 2
    hops_down = nz - 1 - hops_up

    def remote(src, dst, send, recv, to):
        return pltpu.make_async_remote_copy(
            src_ref=src,
            dst_ref=dst,
            send_sem=send,
            recv_sem=recv,
            device_id=to,
            device_id_type=MESH,
        )

    def tile_of(index):
        return pl.ds(pl.multiple_of(index * T, T), T)

    inputs = tuple(
        pltpu.make_async_copy(src, dst, in_sem.at[i])
        for i, (src, dst) in enumerate(
            (
                (dt_in, dt_ref),
                (b_in, b_ref),
                (c_in, c_ref),
                (x_in, x_ref),
                (zg_in, zg_ref),
                (op_in, op_ref),
                (res_in.at[:, tile_of(share)], res_ref),
                (gain_in.at[:, tile_of(share)], gain_ref),
                (rt_in.at[:, tile_of(share)], rt_ref),
            )
        )
    )
    for copy in inputs:
        copy.start()

    barrier = pltpu.get_barrier_semaphore()

    def greet(to):
        pl.semaphore_signal(barrier, inc=1, device_id=to, device_id_type=MESH)

    greet((other, q))
    for o in range(1, gs):
        greet((2 * (group * gs + lax.rem(member + o, gs)) + c, q))
    for o in range(1, ng):
        greet((2 * (lax.rem(group + o, ng) * gs + member) + c, q))

    def greet_plane(o, carry):
        greet((ctx, lax.rem(q + o, nx)))
        return carry

    lax.fori_loop(1, nx, greet_plane, 0)

    @pl.when(member == gs - 1)
    def _():
        greet((up, q))

    @pl.when(member == 0)
    def _():
        greet((down, q))

    share_up = jnp.logical_and(member == gs - 1, 2 * share + c == up)
    share_down = jnp.logical_and(member == 0, 2 * share + c == down)
    near = jnp.logical_or(lax.div(share, gs) == group, lax.rem(share, gs) == member)
    apart = jnp.logical_not(jnp.logical_or(near, jnp.logical_or(share_up, share_down)))

    @pl.when(apart)
    def _():
        greet(opposite)

    keeper = (2 * share + c, z)
    summer = (2 * q + c, lax.rem(z + q, nx))

    @pl.when(jnp.logical_and(q != z, z != 0))
    def _():
        greet(summer)

    peers = (
        (gs + ng + nx - 2)
        + jnp.logical_and(share != z, q != z).astype(jnp.int32)
        + (member == gs - 1).astype(jnp.int32)
        + (member == 0).astype(jnp.int32)
        + apart.astype(jnp.int32)
    )

    mine = pl.ds(pl.multiple_of(c * 64, 64), 64)
    w_local = tuple(
        pltpu.make_async_copy(src, dst, wl_sem.at[i])
        for i, (src, dst) in enumerate(((wg_in, wg_stage), (wu_in, wu_stage), (wd_in, wd_stage)))
    )
    w_sent = tuple(
        remote(w.at[:, mine, :], w.at[:, mine, :], ws_sem.at[i], wr_sem.at[i], (other, q))
        for i, w in enumerate((wgu, wd))
    )

    def pack(e, carry):
        gate, rise, fall = wg_stage[e], wu_stage[e], wd_stage[e]
        wgu[e, mine, 0:384] = gate[:, 0:384]
        wgu[e, mine, 384:768] = rise[:, 0:384]
        wgu[e, mine, 768:896] = jnp.concatenate([gate[:, 384:448], rise[:, 384:448]], axis=1)
        wd[e, mine, 0:384] = fall[:, 0:384]
        wd[e, mine, 384:512] = jnp.concatenate([fall[:, 384:448], fall[:, 384:448]], axis=1)
        return carry

    for copy in w_local:
        copy.start()
    for copy in inputs[0:4]:
        copy.wait()

    lane = lax.broadcasted_iota(jnp.int32, (T, T), 1)
    row = lax.broadcasted_iota(jnp.int32, (T, T), 0)
    left = lane < 64
    upper = row < 64
    row8 = lax.broadcasted_iota(jnp.int32, (8, T), 0)
    dt8[...] = jnp.zeros((8, T), F32)
    dt8[0:4, :] = dt_ref[...]
    steps = jnp.log(1.0 + jnp.exp(dt8[...]))
    rate = jnp.zeros((8, T), F32)
    for h in range(4):
        rate = jnp.where(row8 == h, jnp.exp(jnp.full((8, T), al_ref[h], F32)), rate)
    log_decay = -rate * steps
    before = jnp.where(row <= lane, 1.0, 0.0).astype(BF16)
    ones = jnp.ones((T, T), BF16)
    parts = split3(log_decay)
    running = mm(parts[0], before) + (mm(parts[1], before) + mm(parts[2], before))
    totals = mm(parts[0], ones) + (mm(parts[1], ones) + mm(parts[2], ones))
    carry_w = jnp.exp(totals - running) * steps
    turned = jnp.concatenate([running, carry_w, jnp.zeros((T - 16, T), F32)], axis=0).T
    scores = nt(c_ref[...], b_ref[...])
    inside = []
    states = []
    row16 = lax.broadcasted_iota(jnp.int32, (16, T), 0)

    def log_rows(a0, a1):
        h0, l0 = split2(a0)
        h1, l1 = split2(a1)
        return jnp.where(
            row16 == 0,
            h0.astype(F32),
            jnp.where(
                row16 == 1,
                l0.astype(F32),
                jnp.where(
                    row16 == 2,
                    h1.astype(F32),
                    jnp.where(row16 == 3, l1.astype(F32), 0.0),
                ),
            ),
        ).astype(BF16)

    def unpack(message):
        tail = message[T : T + 16, :].astype(F32)
        return message[0:T, :].astype(F32), tail[0:1] + tail[1:2], tail[2:3] + tail[3:4]

    def spread(a0, a1):
        return jnp.where(upper, jnp.exp(a0), jnp.exp(a1))

    for p in range(2):
        xp = x_ref[:, p * T : (p + 1) * T]
        halves = []
        for h in (2 * p, 2 * p + 1):
            gap = turned[:, h : h + 1] - running[h : h + 1, :]
            weight = jnp.exp(jnp.minimum(gap, 0.0)) * steps[h : h + 1, :]
            hi, lo = split2(jnp.where(row >= lane, scores * weight, 0.0))
            halves.append(mm(hi, xp) + mm(lo, xp))
        inside.append(jnp.where(left, halves[0], halves[1]))
        scale = jnp.where(
            left, turned[:, 8 + 2 * p : 9 + 2 * p], turned[:, 9 + 2 * p : 10 + 2 * p]
        )
        hi, lo = split2((xp.astype(F32) * scale).T)
        states.append(mm(hi, b_ref[...]) + mm(lo, b_ref[...]))

    pl.semaphore_wait(barrier, peers)

    give = jnp.where(c == 0, states[1], states[0])
    keep = jnp.where(c == 0, states[0], states[1])
    a_pairs = [(totals[2 * p : 2 * p + 1, :], totals[2 * p + 1 : 2 * p + 2, :]) for p in range(2)]
    cmsg[0:T, :] = give.astype(BF16)
    cmsg[T : T + 16, :] = log_rows(
        jnp.where(c == 0, a_pairs[1][0], a_pairs[0][0]),
        jnp.where(c == 0, a_pairs[1][1], a_pairs[0][1]),
    )
    to_core = remote(cmsg, crcv, cs_sem.at[0], cr_sem.at[0], (other, q))
    to_core.start()
    own_a0 = jnp.where(c == 0, a_pairs[0][0], a_pairs[1][0])
    own_a1 = jnp.where(c == 0, a_pairs[0][1], a_pairs[1][1])
    to_core.wait_recv()
    got, got_a0, got_a1 = unpack(crcv)
    first = jnp.where(c == 0, keep, got)
    second = jnp.where(c == 0, got, keep)
    first_a0 = jnp.where(c == 0, own_a0, got_a0)
    first_a1 = jnp.where(c == 0, own_a1, got_a1)
    second_a0 = jnp.where(c == 0, got_a0, own_a0)
    second_a1 = jnp.where(c == 0, got_a1, own_a1)
    gbuf[member, 0:T, :] = (spread(second_a0, second_a1) * first + second).astype(BF16)
    gbuf[member, T : T + 16, :] = log_rows(first_a0 + second_a0, first_a1 + second_a1)

    def to_member(o):
        to = 2 * (group * gs + lax.rem(member + o, gs)) + c
        return remote(gbuf.at[member], gbuf.at[member], as_sem.at[o], ar_sem.at[o], (to, q))

    for o in range(1, gs):
        to_member(o).start()
    for copy in w_local:
        copy.wait()
    lax.fori_loop(0, wg_in.shape[0], pack, 0)
    for o in range(1, gs):
        to_member(o).wait_recv()
    zero = jnp.zeros((T, T), F32)
    zero_row = jnp.zeros((1, T), F32)
    total, total_a0, total_a1 = zero, zero_row, zero_row
    part, part_a0, part_a1 = zero, zero_row, zero_row
    for m in range(gs):
        s, a0, a1 = unpack(gbuf.at[m])
        decay = spread(a0, a1)
        total, total_a0, total_a1 = decay * total + s, total_a0 + a0, total_a1 + a1
        earlier = m < member
        part = jnp.where(earlier, decay * part + s, part)
        part_a0 = jnp.where(earlier, part_a0 + a0, part_a0)
        part_a1 = jnp.where(earlier, part_a1 + a1, part_a1)
    tmsg[0:T, :] = total.astype(BF16)
    tmsg[T : T + 16, :] = log_rows(total_a0, total_a1)

    def to_group(o):
        to = 2 * (lax.rem(group + o, ng) * gs + member) + c
        return remote(tmsg, tbuf.at[o], bs_sem.at[o], br_sem.at[o], (to, q))

    for o in range(1, ng):

        @pl.when(group + o < ng)
        def _(o=o):
            to_group(o).start()

    reach = zero
    for o in range(ng - 1, 0, -1):

        @pl.when(group >= o)
        def _(o=o):
            to_group(o).wait_recv()

        @pl.when(group < o)
        def _(o=o):
            tbuf[o] = jnp.zeros((T + 16, T), BF16)

        s, a0, a1 = unpack(tbuf.at[o])
        reach = jnp.where(group >= o, spread(a0, a1) * reach + s, zero)
    at_first = spread(part_a0, part_a1) * reach + part
    at_second = spread(first_a0, first_a1) * at_first + first
    ysnd[...] = jnp.where(c == 0, at_second, at_first).astype(BF16)
    back = remote(ysnd, yrcv, cs_sem.at[1], cr_sem.at[1], (other, q))
    back.start()
    for copy in w_sent:
        copy.start()
    own_in = jnp.where(c == 0, at_first, at_second).astype(BF16)
    back.wait_recv()
    got_in = yrcv[...]
    entering = (
        jnp.where(c == 0, own_in.astype(F32), got_in.astype(F32)).astype(BF16),
        jnp.where(c == 0, got_in.astype(F32), own_in.astype(F32)).astype(BF16),
    )
    for copy in inputs[4:]:
        copy.wait()
    gated = []
    for p in range(2):
        scale = jnp.where(
            left,
            jnp.exp(turned[:, 2 * p : 2 * p + 1]),
            jnp.exp(turned[:, 2 * p + 1 : 2 * p + 2]),
        )
        skip = jnp.where(
            left,
            jnp.full((T, T), dk_ref[2 * p], F32),
            jnp.full((T, T), dk_ref[2 * p + 1], F32),
        )
        xp = x_ref[:, p * T : (p + 1) * T].astype(F32)
        zp = zg_ref[:, p * T : (p + 1) * T].astype(F32)
        out = inside[p] + scale * nt(c_ref[...], entering[p]) + skip * xp
        gated.append((out * silu(zp)).astype(BF16))

    def project(to):
        cols = tile_of(lax.rem(to - z + nx, nx))
        return mm(gated[0], op_ref[0:T, cols]) + mm(gated[1], op_ref[T : 2 * T, cols])

    def send_term(o):
        to = lax.rem(q + o, nx)
        return remote(gt.at[o], rs.at[o], ts_sem.at[o], tr_sem.at[o], (ctx, to))

    def project_step(o, carry):
        gt[o] = project(lax.rem(q + o, nx)).astype(BF16)
        send_term(o).start()
        return carry

    lax.fori_loop(1, nx, project_step, 0)
    own_term = project(q).astype(BF16).astype(F32)
    stream = own_term + res_ref[...].astype(F32)

    def sum_step(o, acc):
        send_term(o).wait_recv()
        return acc + rs[o].astype(F32)

    stream = lax.fori_loop(1, nx, sum_step, stream)
    scaled = (stream * gain_ref[...]).astype(BF16)
    usnd[...] = scaled
    to_opposite = remote(usnd, urcv, us_sem.at[0], ur_sem.at[0], opposite)

    @pl.when(share != z)
    def _():
        to_opposite.start()

    @pl.when(share != z)
    def _():
        to_opposite.wait_recv()
        xs[share] = urcv[...]

    @pl.when(share == z)
    def _():
        xs[share] = usnd[...]

    def send_rows(o):
        to = lax.rem(q + o, nx)
        return remote(xs.at[share], xs.at[share], gs_sem.at[o], gr_sem.at[o], (ctx, to))

    def rows_step(o, carry):
        send_rows(o).start()
        return carry

    early = lax.rem(share - z + nz - hops_up + 1 + nz, nz) < 3

    @pl.when(early)
    def _():
        lax.fori_loop(1, nx, rows_step, 0)

    def rows_ready(d):
        source = lax.rem(d + z, nx)
        o = lax.rem(q - source + nx, nx)

        @pl.when(o != 0)
        def _():
            remote(xs.at[d], xs.at[d], gs_sem.at[o], gr_sem.at[o], (ctx, source)).wait_recv()

    for copy in w_sent:
        copy.wait_recv()

    def partial(d, k):
        return mm(xs[d], wgu[be_ref[k, 2 * d + c]])

    hops = (hops_up, hops_down)

    def goes_up(way, k):
        return (way == 0) == (k == 0)

    def target(way, s, k):
        if goes_up(way, k):
            return lax.rem(z + hops[way] - s + nz, nz)
        return lax.rem(z + nz - hops[way] + s, nz)

    def send_sum(way, s, k):
        return remote(
            rp.at[way, s, k],
            rp.at[way, s + 1, k],
            rs_sem.at[way, s, k],
            rr_sem.at[way, s, k],
            (up if goes_up(way, k) else down, q),
        )

    rows_ready(lax.rem(z + hops_up, nz))
    for far in (1, nz - 1):
        rows_ready(lax.rem(z + hops_up + far, nz))
    for k in range(2):
        for way in range(2):
            rp[way, 0, k] = partial(target(way, 0, k), k).astype(BF16)
            send_sum(way, 0, k).start()

    @pl.when(jnp.logical_not(early))
    def _():
        lax.fori_loop(1, nx, rows_step, 0)

    osnd[...] = stream.astype(BF16)
    stream_home = remote(osnd, orcv, ps_sem.at[0], pr_sem.at[0], home)

    @pl.when(share != q)
    def _():
        stream_home.start()

    logits = nt(scaled, rt_ref[...])
    expert = lax.broadcasted_iota(jnp.int32, (T, rt_ref.shape[0]), 1)
    chosen = jnp.where(expert == be_ref[0, ctx], logits, 0.0)
    refused = jnp.where(expert == be_ref[1, ctx], logits, 0.0)
    difference = jnp.sum(chosen - refused, axis=1, keepdims=True)
    square = jnp.sum(stream * stream, axis=1, keepdims=True)
    columns = jnp.where(lane == 0, square, jnp.where(lane == 1, difference, 0.0))
    ssnd[...] = columns.T[0:8, :]

    def send_stat(o):
        return remote(
            ssnd, srcv.at[o], ss_sem.at[o], sr_sem.at[o], (ctx, lax.rem(q + o, nx))
        )

    def stat_step(o, carry):
        send_stat(o).start()
        return carry

    lax.fori_loop(1, nx, stat_step, 0)

    def sum_hop(way, s, k):
        value = partial(target(way, s, k), k)
        send_sum(way, s - 1, k).wait_recv()
        rp[way, s, k] = (value + rp[way, s, k].astype(F32)).astype(BF16)
        send_sum(way, s, k).start()

    def hop(s, carry):
        rows_ready(lax.rem(z + hops_up + 1 + s, nz))
        rows_ready(lax.rem(z + hops_up - 1 - s + nz, nz))
        for k in range(2):
            for way in range(2):
                sum_hop(way, s, k)
        return carry

    lax.fori_loop(1, hops_down, hop, 0)
    for k in range(2):
        sum_hop(0, hops_down, k)
    rows_ready(z)

    def stat_sum(o, acc):
        send_stat(o).wait_recv()
        return acc + srcv[o]

    stats = lax.fori_loop(1, nx, stat_sum, ssnd[...])
    inverse = lax.rsqrt(stats[0:1, :] * (1.0 / (nx * T)) + epsilon)
    gate0 = 1.0 / (1.0 + jnp.exp(-stats[1:2, :] * inverse))
    gate1 = 1.0 / (1.0 + jnp.exp(stats[1:2, :] * inverse))
    pick = jnp.where(row == 0, inverse, jnp.where(row == 1, gate0, jnp.where(row == 2, gate1, 0.0)))
    turned2 = pick.T
    norm = turned2[:, 0:1]
    hb = (hb0, hb1)

    def source_of(way, s, k):
        return lax.rem(z - s + nz, nz) if goes_up(way, k) else lax.rem(z + s, nz)

    def pass_hidden(way, s, k, source):
        return remote(
            hb[k].at[source],
            hb[k].at[source],
            hs_sem.at[way, s, k],
            hr_sem.at[way, s, k],
            (up if goes_up(way, k) else down, q),
        )

    def send_hidden(way, s, k):
        return pass_hidden(way, s, k, source_of(way, s, k))

    def arrived(way, s, k):
        return pass_hidden(way, s, k, source_of(way, s + 1, k))

    rest0 = None
    own = (partial(z, 0), partial(z, 1))
    for k in range(2):
        value = own[k]
        for way in (1, 0):
            send_sum(way, hops[way] - 1, k).wait_recv()
            value = value + rp[way, hops[way], k].astype(F32)
        value = value * norm
        mix = turned2[:, 1 + k : 2 + k]
        both = value[:, 768:896]
        swapped = pltpu.roll(both, 64, 1)
        main = (silu(value[:, 0:384]) * value[:, 384:768] * mix).astype(BF16)
        if k == 0:
            rest0 = silu(both) * swapped * mix
            hb0[z] = main
        else:
            hb1[z, :, 0:384] = main
            hb1[z, :, 384:512] = jnp.where(left, rest0, silu(swapped) * both * mix).astype(BF16)
        for way in range(2):
            send_hidden(way, 0, k).start()

    def send_out(d):
        to = lax.rem(d + z, nx)
        return remote(os_.at[d], ob.at[q], os_sem.at[d], or_sem.at[q], (ctx, to))

    def finish(d):
        e0 = be_ref[0, 2 * d + c]
        e1 = be_ref[1, 2 * d + c]
        w0 = wd[e0]
        w1 = wd[e1]
        rest = jnp.where(left, w0[:, 384:512].astype(F32), w1[:, 384:512].astype(F32)).astype(BF16)
        value = (
            nt(hb0[d], w0[:, 0:384])
            + nt(hb1[d, :, 0:384], w1[:, 0:384])
            + nt(hb1[d, :, 384:512], rest)
        )
        os_[d] = value.astype(BF16)

        @pl.when(d != share)
        def _():
            send_out(d).start()

    def pass_on(s, first, both):
        for k in range(2):
            arrived(0, s, k).wait_recv()
            send_hidden(0, s + 1, k).start()
            arrived(1, s, k).wait_recv()
            if both:
                send_hidden(1, s + 1, k).start()
            if not first:
                finish(lax.rem(z - s + nz, nz) if k == 0 else lax.rem(z + s, nz))
            elif k == 0:
                finish(z)

    def pass_step(s, carry):
        pass_on(s, False, True)
        return carry

    pass_on(0, True, hops_down > 1)
    if hops_down > 1:
        lax.fori_loop(1, hops_down - 1, pass_step, 0)
        pass_on(hops_down - 1, False, False)
    finish(lax.rem(z - hops_down + nz, nz))
    finish(lax.rem(z + hops_down, nz))
    for k in range(2):
        arrived(0, hops_down, k).wait_recv()
    finish(lax.rem(z + hops_up, nz))

    def out_sum(o, acc):
        source = lax.rem(q + o, nx)
        remote(os_.at[0], ob.at[source], os_sem.at[0], or_sem.at[source], (ctx, source)).wait_recv()
        return acc + ob[source].astype(F32)

    fsnd[...] = lax.fori_loop(1, nx, out_sum, os_[share].astype(F32)).astype(BF16)
    to_keeper = remote(fsnd, frcv, us_sem.at[1], ur_sem.at[1], keeper)
    moved = jnp.logical_or(share != z, q != z)

    @pl.when(moved)
    def _():
        to_keeper.start()

    @pl.when(share != q)
    def _():
        stream_home.wait_recv()
        out_ref[0] = orcv[...].astype(F32)

    @pl.when(share == q)
    def _():
        out_ref[0] = osnd[...].astype(F32)

    @pl.when(moved)
    def _():
        to_keeper.wait_recv()
        out_ref[1] = frcv[...].astype(F32)

    @pl.when(jnp.logical_not(moved))
    def _():
        out_ref[1] = fsnd[...].astype(F32)

    for copy in (*w_sent, to_core, back):
        copy.wait_send()
    for o in range(1, gs):
        to_member(o).wait_send()
    for o in range(1, ng):

        @pl.when(group + o < ng)
        def _(o=o):
            to_group(o).wait_send()

    @pl.when(share != z)
    def _():
        to_opposite.wait_send()

    @pl.when(share != q)
    def _():
        stream_home.wait_send()

    @pl.when(moved)
    def _():
        to_keeper.wait_send()

    def drain(o, carry):
        send_term(o).wait_send()
        send_stat(o).wait_send()
        send_rows(o).wait_send()
        send_out(lax.rem(share + o, nx)).wait_send()
        return carry

    lax.fori_loop(1, nx, drain, 0)

    def drain_up(s, carry):
        for k in range(2):
            send_sum(0, s, k).wait_send()
            send_hidden(0, s, k).wait_send()
        return carry

    def drain_down(s, carry):
        for k in range(2):
            send_sum(1, s, k).wait_send()
            send_hidden(1, s, k).wait_send()
        return carry

    lax.fori_loop(0, hops_up, drain_up, 0)
    lax.fori_loop(0, hops_down, drain_down, 0)


def per_device(
    nz,
    nx,
    gs,
    x_in,
    z_gate,
    b_proj,
    c_proj,
    dt_raw,
    a_log,
    d_skip,
    out_proj,
    residual,
    norm_gain,
    router,
    w_gate,
    w_up,
    w_down,
    block_experts,
):
    experts = w_gate.shape[0]
    wide = 896
    vmem = pl.BlockSpec(memory_space=pltpu.VMEM)
    smem = pl.BlockSpec(memory_space=pltpu.SMEM)
    hbm = pl.BlockSpec(memory_space=pl.ANY)
    dma = pltpu.SemaphoreType.DMA
    hops = nz // 2
    both = pl.pallas_call(
        functools.partial(kernel, nz, nx, gs),
        out_shape=jax.ShapeDtypeStruct((2, T, T), F32),
        in_specs=[
            hbm,
            hbm,
            hbm,
            hbm,
            hbm,
            smem,
            smem,
            hbm,
            hbm,
            hbm,
            hbm,
            hbm,
            hbm,
            hbm,
            smem,
        ],
        out_specs=vmem,
        scratch_shapes=[
            pltpu.VMEM(x_in.shape, BF16),
            pltpu.VMEM(x_in.shape, BF16),
            pltpu.VMEM((T, T), BF16),
            pltpu.VMEM((T, T), BF16),
            pltpu.VMEM(dt_raw.shape, F32),
            pltpu.VMEM(out_proj.shape, BF16),
            pltpu.VMEM((T, T), BF16),
            pltpu.VMEM((1, T), F32),
            pltpu.VMEM((experts, T), BF16),
            pltpu.VMEM((8, T), F32),
            pltpu.VMEM(w_gate.shape, BF16),
            pltpu.VMEM(w_gate.shape, BF16),
            pltpu.VMEM(w_gate.shape, BF16),
            pltpu.VMEM((experts, T, wide), BF16),
            pltpu.VMEM((experts, T, 512), BF16),
            pltpu.VMEM((T + 16, T), BF16),
            pltpu.VMEM((T + 16, T), BF16),
            pltpu.VMEM((gs, T + 16, T), BF16),
            pltpu.VMEM((T + 16, T), BF16),
            pltpu.VMEM((nz // gs, T + 16, T), BF16),
            pltpu.VMEM((T, T), BF16),
            pltpu.VMEM((T, T), BF16),
            pltpu.VMEM((nx, T, T), BF16),
            pltpu.VMEM((nx, T, T), BF16),
            pltpu.VMEM((T, T), BF16),
            pltpu.VMEM((T, T), BF16),
            pltpu.VMEM((nx, T, T), BF16),
            pltpu.VMEM((8, T), F32),
            pltpu.VMEM((nx, 8, T), F32),
            pltpu.VMEM((2, hops + 1, 2, T, wide), BF16),
            pltpu.VMEM((nz, T, 384), BF16),
            pltpu.VMEM((nz, T, 512), BF16),
            pltpu.VMEM((nx, T, T), BF16),
            pltpu.VMEM((nx, T, T), BF16),
            pltpu.VMEM((T, T), BF16),
            pltpu.VMEM((T, T), BF16),
            pltpu.VMEM((T, T), BF16),
            pltpu.VMEM((T, T), BF16),
            dma((9,)),
            dma((3,)),
            dma((2,)),
            dma((2,)),
            dma((2,)),
            dma((2,)),
            dma((gs,)),
            dma((gs,)),
            dma((nz // gs,)),
            dma((nz // gs,)),
            dma((nx,)),
            dma((nx,)),
            dma((nx,)),
            dma((nx,)),
            dma((2,)),
            dma((2,)),
            dma((2,)),
            dma((2,)),
            dma((nx,)),
            dma((nx,)),
            dma((2, hops, 2)),
            dma((2, hops, 2)),
            dma((2, hops, 2)),
            dma((2, hops, 2)),
            dma((nx,)),
            dma((nx,)),
        ],
        compiler_params=pltpu.CompilerParams(
            collective_id=0, has_side_effects=True, vmem_limit_bytes=60 * 2**20
        ),
    )(
        x_in,
        z_gate,
        b_proj,
        c_proj,
        dt_raw,
        a_log,
        d_skip,
        out_proj,
        residual,
        norm_gain.reshape(1, -1),
        router.T,
        w_gate,
        w_up,
        w_down,
        block_experts.T,
    )
    return both[0].astype(BF16), both[1].astype(BF16)


def solution(mesh):
    nz = mesh.shape["ctx"] // 2
    nx = mesh.shape["exp"]
    gs = 4 if nz >= 16 else 2
    placed = (
        P("ctx", "exp"),
        P("ctx", "exp"),
        P("ctx", None),
        P("ctx", None),
        P("exp", "ctx"),
        P("exp"),
        P("exp"),
        P("exp", None),
        P("ctx", None),
        P(),
        P(),
        P(None, "ctx", "exp"),
        P(None, "ctx", "exp"),
        P(None, "ctx", "exp"),
        P(),
    )
    return jax.shard_map(
        functools.partial(per_device, nz, nx, gs),
        mesh=mesh,
        in_specs=placed,
        out_specs=(P("ctx", "exp"), P("ctx", "exp")),
        check_vma=False,
    )
```

```python
import functools

import jax
import jax.numpy as jnp
from jax import lax
from jax.experimental import pallas as pl
from jax.experimental.pallas import tpu as pltpu
from jax.sharding import PartitionSpec as P

MESH = pl.DeviceIdType.MESH
F32 = jnp.float32
BF16 = jnp.bfloat16
T = 128
epsilon = 1e-05


def mm(a, b):
    return jnp.dot(a, b, preferred_element_type=F32)


def nt(a, b):
    return lax.dot_general(a, b, (((1,), (1,)), ((), ())), preferred_element_type=F32)


def split2(v):
    hi = v.astype(BF16)
    return hi, (v - hi.astype(F32)).astype(BF16)


def split3(v):
    hi = v.astype(BF16)
    rest = v - hi.astype(F32)
    mid = rest.astype(BF16)
    return hi, mid, (rest - mid.astype(F32)).astype(BF16)


def silu(v):
    return v / (1.0 + jnp.exp(-v))


def kernel(
    nz,
    nx,
    gs,
    x_in,
    zg_in,
    b_in,
    c_in,
    dt_in,
    al_ref,
    dk_ref,
    op_in,
    res_in,
    gain_in,
    rt_in,
    wg_in,
    wu_in,
    wd_in,
    be_ref,
    out_ref,
    x_ref,
    zg_ref,
    b_ref,
    c_ref,
    dt_ref,
    op_ref,
    res_ref,
    gain_ref,
    rt_ref,
    dt8,
    wg_stage,
    wu_stage,
    wd_stage,
    wgu,
    wd,
    cmsg,
    crcv,
    gbuf,
    tmsg,
    tbuf,
    entry,
    shared,
    ysnd,
    yrcv,
    gt,
    rs,
    usnd,
    urcv,
    xs,
    ssnd,
    srcv,
    rp,
    hb0,
    hb1,
    os_,
    ob,
    fsnd,
    frcv,
    osnd,
    orcv,
    in_sem,
    wl_sem,
    ws_sem,
    wr_sem,
    cs_sem,
    cr_sem,
    as_sem,
    ar_sem,
    bs_sem,
    br_sem,
    es_sem,
    er_sem,
    ts_sem,
    tr_sem,
    ss_sem,
    sr_sem,
    us_sem,
    ur_sem,
    ps_sem,
    pr_sem,
    gs_sem,
    gr_sem,
    rs_sem,
    rr_sem,
    hs_sem,
    hr_sem,
    os_sem,
    or_sem,
):
    ctx = lax.axis_index("ctx")
    q = lax.axis_index("exp")
    z = lax.div(ctx, 2)
    c = lax.rem(ctx, 2)
    ng = nz // gs
    member = lax.rem(z, gs)
    group = lax.div(z, gs)
    up = 2 * lax.rem(z + 1, nz) + c
    down = 2 * lax.rem(z + nz - 1, nz) + c
    other = 2 * z + (1 - c)
    share = lax.rem(q - z + nx, nx)
    opposite = (2 * share + c, q)
    home = (ctx, share)
    hops_up = nz // 2
    hops_down = nz - 1 - hops_up

    def remote(src, dst, send, recv, to):
        return pltpu.make_async_remote_copy(
            src_ref=src,
            dst_ref=dst,
            send_sem=send,
            recv_sem=recv,
            device_id=to,
            device_id_type=MESH,
        )

    def tile_of(index):
        return pl.ds(pl.multiple_of(index * T, T), T)

    inputs = tuple(
        pltpu.make_async_copy(src, dst, in_sem.at[i])
        for i, (src, dst) in enumerate(
            (
                (dt_in, dt_ref),
                (b_in, b_ref),
                (c_in, c_ref),
                (x_in, x_ref),
                (zg_in, zg_ref),
                (op_in, op_ref),
                (res_in.at[:, tile_of(share)], res_ref),
                (gain_in.at[:, tile_of(share)], gain_ref),
                (rt_in.at[:, tile_of(share)], rt_ref),
            )
        )
    )
    for copy in inputs:
        copy.start()

    barrier = pltpu.get_barrier_semaphore()

    def greet(to):
        pl.semaphore_signal(barrier, inc=1, device_id=to, device_id_type=MESH)

    greet((other, q))
    for o in range(1, gs):
        greet((2 * (group * gs + lax.rem(member + o, gs)) + c, q))
    for o in range(1, ng):
        greet((2 * (lax.rem(group + o, ng) * gs + member) + c, q))

    def greet_plane(o, carry):
        greet((ctx, lax.rem(q + o, nx)))
        return carry

    lax.fori_loop(1, nx, greet_plane, 0)

    @pl.when(member == gs - 1)
    def _():
        greet((up, q))

    @pl.when(member == 0)
    def _():
        greet((down, q))

    share_up = jnp.logical_and(member == gs - 1, 2 * share + c == up)
    share_down = jnp.logical_and(member == 0, 2 * share + c == down)
    near = jnp.logical_or(lax.div(share, gs) == group, lax.rem(share, gs) == member)
    apart = jnp.logical_not(jnp.logical_or(near, jnp.logical_or(share_up, share_down)))

    @pl.when(apart)
    def _():
        greet(opposite)

    keeper = (2 * share + c, z)
    summer = (2 * q + c, lax.rem(z + q, nx))

    @pl.when(jnp.logical_and(q != z, z != 0))
    def _():
        greet(summer)

    peers = (
        (gs + ng + nx - 2)
        + jnp.logical_and(share != z, q != z).astype(jnp.int32)
        + (member == gs - 1).astype(jnp.int32)
        + (member == 0).astype(jnp.int32)
        + apart.astype(jnp.int32)
    )

    mine = pl.ds(pl.multiple_of(c * 64, 64), 64)
    w_local = tuple(
        pltpu.make_async_copy(src, dst, wl_sem.at[i])
        for i, (src, dst) in enumerate(((wg_in, wg_stage), (wu_in, wu_stage), (wd_in, wd_stage)))
    )
    w_sent = tuple(
        remote(w.at[:, mine, :], w.at[:, mine, :], ws_sem.at[i], wr_sem.at[i], (other, q))
        for i, w in enumerate((wgu, wd))
    )

    def pack(e, carry):
        gate, rise, fall = wg_stage[e], wu_stage[e], wd_stage[e]
        wgu[e, mine, 0:384] = gate[:, 0:384]
        wgu[e, mine, 384:768] = rise[:, 0:384]
        wgu[e, mine, 768:896] = jnp.concatenate([gate[:, 384:448], rise[:, 384:448]], axis=1)
        wd[e, mine, 0:384] = fall[:, 0:384]
        wd[e, mine, 384:512] = jnp.concatenate([fall[:, 384:448], fall[:, 384:448]], axis=1)
        return carry

    for copy in w_local:
        copy.start()
    for copy in inputs[0:4]:
        copy.wait()

    lane = lax.broadcasted_iota(jnp.int32, (T, T), 1)
    row = lax.broadcasted_iota(jnp.int32, (T, T), 0)
    left = lane < 64
    upper = row < 64
    row8 = lax.broadcasted_iota(jnp.int32, (8, T), 0)
    dt8[...] = jnp.zeros((8, T), F32)
    dt8[0:4, :] = dt_ref[...]
    steps = jnp.log(1.0 + jnp.exp(dt8[...]))
    rate = jnp.zeros((8, T), F32)
    for h in range(4):
        rate = jnp.where(row8 == h, jnp.exp(jnp.full((8, T), al_ref[h], F32)), rate)
    log_decay = -rate * steps
    before = jnp.where(row <= lane, 1.0, 0.0).astype(BF16)
    ones = jnp.ones((T, T), BF16)
    parts = split3(log_decay)
    running = mm(parts[0], before) + (mm(parts[1], before) + mm(parts[2], before))
    totals = mm(parts[0], ones) + (mm(parts[1], ones) + mm(parts[2], ones))
    carry_w = jnp.exp(totals - running) * steps
    turned = jnp.concatenate([running, carry_w, jnp.zeros((T - 16, T), F32)], axis=0).T
    scores = nt(c_ref[...], b_ref[...])
    inside = []
    states = []
    row16 = lax.broadcasted_iota(jnp.int32, (16, T), 0)

    def log_rows(a0, a1):
        h0, l0 = split2(a0)
        h1, l1 = split2(a1)
        return jnp.where(
            row16 == 0,
            h0.astype(F32),
            jnp.where(
                row16 == 1,
                l0.astype(F32),
                jnp.where(
                    row16 == 2,
                    h1.astype(F32),
                    jnp.where(row16 == 3, l1.astype(F32), 0.0),
                ),
            ),
        ).astype(BF16)

    def unpack(message):
        tail = message[T : T + 16, :].astype(F32)
        return message[0:T, :].astype(F32), tail[0:1] + tail[1:2], tail[2:3] + tail[3:4]

    def spread(a0, a1):
        return jnp.where(upper, jnp.exp(a0), jnp.exp(a1))

    for p in range(2):
        xp = x_ref[:, p * T : (p + 1) * T]
        halves = []
        for h in (2 * p, 2 * p + 1):
            gap = turned[:, h : h + 1] - running[h : h + 1, :]
            weight = jnp.exp(jnp.minimum(gap, 0.0)) * steps[h : h + 1, :]
            hi, lo = split2(jnp.where(row >= lane, scores * weight, 0.0))
            halves.append(mm(hi, xp) + mm(lo, xp))
        inside.append(jnp.where(left, halves[0], halves[1]))
        scale = jnp.where(
            left, turned[:, 8 + 2 * p : 9 + 2 * p], turned[:, 9 + 2 * p : 10 + 2 * p]
        )
        hi, lo = split2((xp.astype(F32) * scale).T)
        states.append(mm(hi, b_ref[...]) + mm(lo, b_ref[...]))

    pl.semaphore_wait(barrier, peers)

    give = jnp.where(c == 0, states[1], states[0])
    keep = jnp.where(c == 0, states[0], states[1])
    a_pairs = [(totals[2 * p : 2 * p + 1, :], totals[2 * p + 1 : 2 * p + 2, :]) for p in range(2)]
    cmsg[0:T, :] = give.astype(BF16)
    cmsg[T : T + 16, :] = log_rows(
        jnp.where(c == 0, a_pairs[1][0], a_pairs[0][0]),
        jnp.where(c == 0, a_pairs[1][1], a_pairs[0][1]),
    )
    to_core = remote(cmsg, crcv, cs_sem.at[0], cr_sem.at[0], (other, q))
    to_core.start()
    own_a0 = jnp.where(c == 0, a_pairs[0][0], a_pairs[1][0])
    own_a1 = jnp.where(c == 0, a_pairs[0][1], a_pairs[1][1])
    to_core.wait_recv()
    got, got_a0, got_a1 = unpack(crcv)
    first = jnp.where(c == 0, keep, got)
    second = jnp.where(c == 0, got, keep)
    first_a0 = jnp.where(c == 0, own_a0, got_a0)
    first_a1 = jnp.where(c == 0, own_a1, got_a1)
    second_a0 = jnp.where(c == 0, got_a0, own_a0)
    second_a1 = jnp.where(c == 0, got_a1, own_a1)
    gbuf[member, 0:T, :] = (spread(second_a0, second_a1) * first + second).astype(BF16)
    gbuf[member, T : T + 16, :] = log_rows(first_a0 + second_a0, first_a1 + second_a1)

    def to_member(o):
        to = 2 * (group * gs + lax.rem(member + o, gs)) + c
        return remote(gbuf.at[member], gbuf.at[member], as_sem.at[o], ar_sem.at[o], (to, q))

    for o in range(1, gs):
        to_member(o).start()
    for copy in w_local:
        copy.wait()
    lax.fori_loop(0, wg_in.shape[0], pack, 0)
    for o in range(1, gs):
        to_member(o).wait_recv()
    zero = jnp.zeros((T, T), F32)
    zero_row = jnp.zeros((1, T), F32)
    total, total_a0, total_a1 = zero, zero_row, zero_row
    part, part_a0, part_a1 = zero, zero_row, zero_row
    for m in range(gs):
        s, a0, a1 = unpack(gbuf.at[m])
        decay = spread(a0, a1)
        total, total_a0, total_a1 = decay * total + s, total_a0 + a0, total_a1 + a1
        earlier = m < member
        part = jnp.where(earlier, decay * part + s, part)
        part_a0 = jnp.where(earlier, part_a0 + a0, part_a0)
        part_a1 = jnp.where(earlier, part_a1 + a1, part_a1)
    some = T // gs
    own_rows = pl.ds(pl.multiple_of(member * some, some), some)
    entry[...] = total.astype(BF16)
    tmsg[0:some, :] = entry[own_rows, :]
    tmsg[some : some + 16, :] = log_rows(total_a0, total_a1)

    def to_group(o):
        to = 2 * (lax.rem(group + o, ng) * gs + member) + c
        return remote(tmsg, tbuf.at[o], bs_sem.at[o], br_sem.at[o], (to, q))

    for o in range(1, ng):

        @pl.when(group + o < ng)
        def _(o=o):
            to_group(o).start()

    reach = jnp.zeros((some, T), F32)
    for o in range(ng - 1, 0, -1):

        @pl.when(group >= o)
        def _(o=o):
            to_group(o).wait_recv()

        @pl.when(group < o)
        def _(o=o):
            tbuf[o] = jnp.zeros((some + 16, T), BF16)

        tail = tbuf[o, some : some + 16, :].astype(F32)
        log_total = jnp.where(member < gs // 2, tail[0:1] + tail[1:2], tail[2:3] + tail[3:4])
        reach = jnp.exp(log_total) * reach + tbuf[o, 0:some, :].astype(F32)
    shared[own_rows, :] = reach.astype(BF16)

    def share_rows(o):
        to = 2 * (group * gs + lax.rem(member + o, gs)) + c
        rows = shared.at[own_rows, :]
        return remote(rows, rows, es_sem.at[o], er_sem.at[o], (to, q))

    for o in range(1, gs):
        share_rows(o).start()
    for o in range(1, gs):
        share_rows(o).wait_recv()
    reach = shared[...].astype(F32)
    at_first = spread(part_a0, part_a1) * reach + part
    at_second = spread(first_a0, first_a1) * at_first + first
    ysnd[...] = jnp.where(c == 0, at_second, at_first).astype(BF16)
    back = remote(ysnd, yrcv, cs_sem.at[1], cr_sem.at[1], (other, q))
    back.start()
    for copy in w_sent:
        copy.start()
    own_in = jnp.where(c == 0, at_first, at_second).astype(BF16)
    back.wait_recv()
    got_in = yrcv[...]
    entering = (
        jnp.where(c == 0, own_in.astype(F32), got_in.astype(F32)).astype(BF16),
        jnp.where(c == 0, got_in.astype(F32), own_in.astype(F32)).astype(BF16),
    )
    for copy in inputs[4:]:
        copy.wait()
    gated = []
    for p in range(2):
        scale = jnp.where(
            left,
            jnp.exp(turned[:, 2 * p : 2 * p + 1]),
            jnp.exp(turned[:, 2 * p + 1 : 2 * p + 2]),
        )
        skip = jnp.where(
            left,
            jnp.full((T, T), dk_ref[2 * p], F32),
            jnp.full((T, T), dk_ref[2 * p + 1], F32),
        )
        xp = x_ref[:, p * T : (p + 1) * T].astype(F32)
        zp = zg_ref[:, p * T : (p + 1) * T].astype(F32)
        out = inside[p] + scale * nt(c_ref[...], entering[p]) + skip * xp
        gated.append((out * silu(zp)).astype(BF16))

    def project(to):
        cols = tile_of(lax.rem(to - z + nx, nx))
        return mm(gated[0], op_ref[0:T, cols]) + mm(gated[1], op_ref[T : 2 * T, cols])

    def send_term(o):
        to = lax.rem(q + o, nx)
        return remote(gt.at[o], rs.at[o], ts_sem.at[o], tr_sem.at[o], (ctx, to))

    def project_step(o, carry):
        gt[o] = project(lax.rem(q + o, nx)).astype(BF16)
        send_term(o).start()
        return carry

    lax.fori_loop(1, nx, project_step, 0)
    own_term = project(q).astype(BF16).astype(F32)
    stream = own_term + res_ref[...].astype(F32)

    def sum_step(o, acc):
        send_term(o).wait_recv()
        return acc + rs[o].astype(F32)

    stream = lax.fori_loop(1, nx, sum_step, stream)
    scaled = (stream * gain_ref[...]).astype(BF16)
    usnd[...] = scaled
    to_opposite = remote(usnd, urcv, us_sem.at[0], ur_sem.at[0], opposite)

    @pl.when(share != z)
    def _():
        to_opposite.start()

    @pl.when(share != z)
    def _():
        to_opposite.wait_recv()
        xs[share] = urcv[...]

    @pl.when(share == z)
    def _():
        xs[share] = usnd[...]

    def send_rows(o):
        to = lax.rem(q + o, nx)
        return remote(xs.at[share], xs.at[share], gs_sem.at[o], gr_sem.at[o], (ctx, to))

    def rows_step(o, carry):
        send_rows(o).start()
        return carry

    early = lax.rem(share - z + nz - hops_up + 1 + nz, nz) < 3

    @pl.when(early)
    def _():
        lax.fori_loop(1, nx, rows_step, 0)

    def rows_ready(d):
        source = lax.rem(d + z, nx)
        o = lax.rem(q - source + nx, nx)

        @pl.when(o != 0)
        def _():
            remote(xs.at[d], xs.at[d], gs_sem.at[o], gr_sem.at[o], (ctx, source)).wait_recv()

    for copy in w_sent:
        copy.wait_recv()

    def partial(d, k):
        return mm(xs[d], wgu[be_ref[k, 2 * d + c]])

    hops = (hops_up, hops_down)

    def goes_up(way, k):
        return (way == 0) == (k == 0)

    def target(way, s, k):
        if goes_up(way, k):
            return lax.rem(z + hops[way] - s + nz, nz)
        return lax.rem(z + nz - hops[way] + s, nz)

    def send_sum(way, s, k):
        return remote(
            rp.at[way, s, k],
            rp.at[way, s + 1, k],
            rs_sem.at[way, s, k],
            rr_sem.at[way, s, k],
            (up if goes_up(way, k) else down, q),
        )

    rows_ready(lax.rem(z + hops_up, nz))
    for far in (1, nz - 1):
        rows_ready(lax.rem(z + hops_up + far, nz))
    for k in range(2):
        for way in range(2):
            rp[way, 0, k] = partial(target(way, 0, k), k).astype(BF16)
            send_sum(way, 0, k).start()

    @pl.when(jnp.logical_not(early))
    def _():
        lax.fori_loop(1, nx, rows_step, 0)

    osnd[...] = stream.astype(BF16)
    stream_home = remote(osnd, orcv, ps_sem.at[0], pr_sem.at[0], home)

    @pl.when(share != q)
    def _():
        stream_home.start()

    logits = nt(scaled, rt_ref[...])
    expert = lax.broadcasted_iota(jnp.int32, (T, rt_ref.shape[0]), 1)
    chosen = jnp.where(expert == be_ref[0, ctx], logits, 0.0)
    refused = jnp.where(expert == be_ref[1, ctx], logits, 0.0)
    difference = jnp.sum(chosen - refused, axis=1, keepdims=True)
    square = jnp.sum(stream * stream, axis=1, keepdims=True)
    columns = jnp.where(lane == 0, square, jnp.where(lane == 1, difference, 0.0))
    ssnd[...] = columns.T[0:8, :]

    def send_stat(o):
        return remote(
            ssnd, srcv.at[o], ss_sem.at[o], sr_sem.at[o], (ctx, lax.rem(q + o, nx))
        )

    def stat_step(o, carry):
        send_stat(o).start()
        return carry

    lax.fori_loop(1, nx, stat_step, 0)

    def sum_hop(way, s, k):
        value = partial(target(way, s, k), k)
        send_sum(way, s - 1, k).wait_recv()
        rp[way, s, k] = (value + rp[way, s, k].astype(F32)).astype(BF16)
        send_sum(way, s, k).start()

    def hop(s, carry):
        rows_ready(lax.rem(z + hops_up + 1 + s, nz))
        rows_ready(lax.rem(z + hops_up - 1 - s + nz, nz))
        for k in range(2):
            for way in range(2):
                sum_hop(way, s, k)
        return carry

    lax.fori_loop(1, hops_down, hop, 0)
    for k in range(2):
        sum_hop(0, hops_down, k)
    rows_ready(z)

    def stat_sum(o, acc):
        send_stat(o).wait_recv()
        return acc + srcv[o]

    stats = lax.fori_loop(1, nx, stat_sum, ssnd[...])
    inverse = lax.rsqrt(stats[0:1, :] * (1.0 / (nx * T)) + epsilon)
    gate0 = 1.0 / (1.0 + jnp.exp(-stats[1:2, :] * inverse))
    gate1 = 1.0 / (1.0 + jnp.exp(stats[1:2, :] * inverse))
    pick = jnp.where(row == 0, inverse, jnp.where(row == 1, gate0, jnp.where(row == 2, gate1, 0.0)))
    turned2 = pick.T
    norm = turned2[:, 0:1]
    hb = (hb0, hb1)

    def source_of(way, s, k):
        return lax.rem(z - s + nz, nz) if goes_up(way, k) else lax.rem(z + s, nz)

    def pass_hidden(way, s, k, source):
        return remote(
            hb[k].at[source],
            hb[k].at[source],
            hs_sem.at[way, s, k],
            hr_sem.at[way, s, k],
            (up if goes_up(way, k) else down, q),
        )

    def send_hidden(way, s, k):
        return pass_hidden(way, s, k, source_of(way, s, k))

    def arrived(way, s, k):
        return pass_hidden(way, s, k, source_of(way, s + 1, k))

    rest0 = None
    own = (partial(z, 0), partial(z, 1))
    for k in range(2):
        value = own[k]
        for way in (1, 0):
            send_sum(way, hops[way] - 1, k).wait_recv()
            value = value + rp[way, hops[way], k].astype(F32)
        value = value * norm
        mix = turned2[:, 1 + k : 2 + k]
        both = value[:, 768:896]
        swapped = pltpu.roll(both, 64, 1)
        main = (silu(value[:, 0:384]) * value[:, 384:768] * mix).astype(BF16)
        if k == 0:
            rest0 = silu(both) * swapped * mix
            hb0[z] = main
        else:
            hb1[z, :, 0:384] = main
            hb1[z, :, 384:512] = jnp.where(left, rest0, silu(swapped) * both * mix).astype(BF16)
        for way in range(2):
            send_hidden(way, 0, k).start()

    def send_out(d):
        to = lax.rem(d + z, nx)
        return remote(os_.at[d], ob.at[q], os_sem.at[d], or_sem.at[q], (ctx, to))

    def finish(d):
        e0 = be_ref[0, 2 * d + c]
        e1 = be_ref[1, 2 * d + c]
        w0 = wd[e0]
        w1 = wd[e1]
        rest = jnp.where(left, w0[:, 384:512].astype(F32), w1[:, 384:512].astype(F32)).astype(BF16)
        value = (
            nt(hb0[d], w0[:, 0:384])
            + nt(hb1[d, :, 0:384], w1[:, 0:384])
            + nt(hb1[d, :, 384:512], rest)
        )
        os_[d] = value.astype(BF16)

        @pl.when(d != share)
        def _():
            send_out(d).start()

    def pass_on(s, first, both):
        for k in range(2):
            arrived(0, s, k).wait_recv()
            send_hidden(0, s + 1, k).start()
            arrived(1, s, k).wait_recv()
            if both:
                send_hidden(1, s + 1, k).start()
            if not first:
                finish(lax.rem(z - s + nz, nz) if k == 0 else lax.rem(z + s, nz))
            elif k == 0:
                finish(z)

    def pass_step(s, carry):
        pass_on(s, False, True)
        return carry

    pass_on(0, True, hops_down > 1)
    if hops_down > 1:
        lax.fori_loop(1, hops_down - 1, pass_step, 0)
        pass_on(hops_down - 1, False, False)
    finish(lax.rem(z - hops_down + nz, nz))
    finish(lax.rem(z + hops_down, nz))
    for k in range(2):
        arrived(0, hops_down, k).wait_recv()
    finish(lax.rem(z + hops_up, nz))

    def out_sum(o, acc):
        source = lax.rem(q + o, nx)
        remote(os_.at[0], ob.at[source], os_sem.at[0], or_sem.at[source], (ctx, source)).wait_recv()
        return acc + ob[source].astype(F32)

    fsnd[...] = lax.fori_loop(1, nx, out_sum, os_[share].astype(F32)).astype(BF16)
    to_keeper = remote(fsnd, frcv, us_sem.at[1], ur_sem.at[1], keeper)
    moved = jnp.logical_or(share != z, q != z)

    @pl.when(moved)
    def _():
        to_keeper.start()

    @pl.when(share != q)
    def _():
        stream_home.wait_recv()
        out_ref[0] = orcv[...].astype(F32)

    @pl.when(share == q)
    def _():
        out_ref[0] = osnd[...].astype(F32)

    @pl.when(moved)
    def _():
        to_keeper.wait_recv()
        out_ref[1] = frcv[...].astype(F32)

    @pl.when(jnp.logical_not(moved))
    def _():
        out_ref[1] = fsnd[...].astype(F32)

    for copy in (*w_sent, to_core, back):
        copy.wait_send()
    for o in range(1, gs):
        to_member(o).wait_send()
        share_rows(o).wait_send()
    for o in range(1, ng):

        @pl.when(group + o < ng)
        def _(o=o):
            to_group(o).wait_send()

    @pl.when(share != z)
    def _():
        to_opposite.wait_send()

    @pl.when(share != q)
    def _():
        stream_home.wait_send()

    @pl.when(moved)
    def _():
        to_keeper.wait_send()

    def drain(o, carry):
        send_term(o).wait_send()
        send_stat(o).wait_send()
        send_rows(o).wait_send()
        send_out(lax.rem(share + o, nx)).wait_send()
        return carry

    lax.fori_loop(1, nx, drain, 0)

    def drain_up(s, carry):
        for k in range(2):
            send_sum(0, s, k).wait_send()
            send_hidden(0, s, k).wait_send()
        return carry

    def drain_down(s, carry):
        for k in range(2):
            send_sum(1, s, k).wait_send()
            send_hidden(1, s, k).wait_send()
        return carry

    lax.fori_loop(0, hops_up, drain_up, 0)
    lax.fori_loop(0, hops_down, drain_down, 0)


def per_device(
    nz,
    nx,
    gs,
    x_in,
    z_gate,
    b_proj,
    c_proj,
    dt_raw,
    a_log,
    d_skip,
    out_proj,
    residual,
    norm_gain,
    router,
    w_gate,
    w_up,
    w_down,
    block_experts,
):
    experts = w_gate.shape[0]
    wide = 896
    vmem = pl.BlockSpec(memory_space=pltpu.VMEM)
    smem = pl.BlockSpec(memory_space=pltpu.SMEM)
    hbm = pl.BlockSpec(memory_space=pl.ANY)
    dma = pltpu.SemaphoreType.DMA
    hops = nz // 2
    both = pl.pallas_call(
        functools.partial(kernel, nz, nx, gs),
        out_shape=jax.ShapeDtypeStruct((2, T, T), F32),
        in_specs=[
            hbm,
            hbm,
            hbm,
            hbm,
            hbm,
            smem,
            smem,
            hbm,
            hbm,
            hbm,
            hbm,
            hbm,
            hbm,
            hbm,
            smem,
        ],
        out_specs=vmem,
        scratch_shapes=[
            pltpu.VMEM(x_in.shape, BF16),
            pltpu.VMEM(x_in.shape, BF16),
            pltpu.VMEM((T, T), BF16),
            pltpu.VMEM((T, T), BF16),
            pltpu.VMEM(dt_raw.shape, F32),
            pltpu.VMEM(out_proj.shape, BF16),
            pltpu.VMEM((T, T), BF16),
            pltpu.VMEM((1, T), F32),
            pltpu.VMEM((experts, T), BF16),
            pltpu.VMEM((8, T), F32),
            pltpu.VMEM(w_gate.shape, BF16),
            pltpu.VMEM(w_gate.shape, BF16),
            pltpu.VMEM(w_gate.shape, BF16),
            pltpu.VMEM((experts, T, wide), BF16),
            pltpu.VMEM((experts, T, 512), BF16),
            pltpu.VMEM((T + 16, T), BF16),
            pltpu.VMEM((T + 16, T), BF16),
            pltpu.VMEM((gs, T + 16, T), BF16),
            pltpu.VMEM((T // gs + 16, T), BF16),
            pltpu.VMEM((nz // gs, T // gs + 16, T), BF16),
            pltpu.VMEM((T, T), BF16),
            pltpu.VMEM((T, T), BF16),
            pltpu.VMEM((T, T), BF16),
            pltpu.VMEM((T, T), BF16),
            pltpu.VMEM((nx, T, T), BF16),
            pltpu.VMEM((nx, T, T), BF16),
            pltpu.VMEM((T, T), BF16),
            pltpu.VMEM((T, T), BF16),
            pltpu.VMEM((nx, T, T), BF16),
            pltpu.VMEM((8, T), F32),
            pltpu.VMEM((nx, 8, T), F32),
            pltpu.VMEM((2, hops + 1, 2, T, wide), BF16),
            pltpu.VMEM((nz, T, 384), BF16),
            pltpu.VMEM((nz, T, 512), BF16),
            pltpu.VMEM((nx, T, T), BF16),
            pltpu.VMEM((nx, T, T), BF16),
            pltpu.VMEM((T, T), BF16),
            pltpu.VMEM((T, T), BF16),
            pltpu.VMEM((T, T), BF16),
            pltpu.VMEM((T, T), BF16),
            dma((9,)),
            dma((3,)),
            dma((2,)),
            dma((2,)),
            dma((2,)),
            dma((2,)),
            dma((gs,)),
            dma((gs,)),
            dma((nz // gs,)),
            dma((nz // gs,)),
            dma((gs,)),
            dma((gs,)),
            dma((nx,)),
            dma((nx,)),
            dma((nx,)),
            dma((nx,)),
            dma((2,)),
            dma((2,)),
            dma((2,)),
            dma((2,)),
            dma((nx,)),
            dma((nx,)),
            dma((2, hops, 2)),
            dma((2, hops, 2)),
            dma((2, hops, 2)),
            dma((2, hops, 2)),
            dma((nx,)),
            dma((nx,)),
        ],
        compiler_params=pltpu.CompilerParams(
            collective_id=0, has_side_effects=True, vmem_limit_bytes=60 * 2**20
        ),
    )(
        x_in,
        z_gate,
        b_proj,
        c_proj,
        dt_raw,
        a_log,
        d_skip,
        out_proj,
        residual,
        norm_gain.reshape(1, -1),
        router.T,
        w_gate,
        w_up,
        w_down,
        block_experts.T,
    )
    return both[0].astype(BF16), both[1].astype(BF16)


def solution(mesh):
    nz = mesh.shape["ctx"] // 2
    nx = mesh.shape["exp"]
    gs = 4 if nz >= 16 else 2
    placed = (
        P("ctx", "exp"),
        P("ctx", "exp"),
        P("ctx", None),
        P("ctx", None),
        P("exp", "ctx"),
        P("exp"),
        P("exp"),
        P("exp", None),
        P("ctx", None),
        P(),
        P(),
        P(None, "ctx", "exp"),
        P(None, "ctx", "exp"),
        P(None, "ctx", "exp"),
        P(),
    )
    return jax.shard_map(
        functools.partial(per_device, nz, nx, gs),
        mesh=mesh,
        in_specs=placed,
        out_specs=(P("ctx", "exp"), P("ctx", "exp")),
        check_vma=False,
    )
```
